128 devices in a mesh: dp: 32 (over x, z, core), group: 4 (over y).
Axes of the slice: x: 4, y: 4, z: 4, core: 2. Of those that a mesh axis runs over, the one named last changes fastest.
Arguments:
- query_inner: bfloat16 [1024, 32, 3072], P(('dp', 'group')), may hold values from -6 to 6
- query_resid: bfloat16 [1024, 32, 768], P(('dp', 'group')), may hold values from -6 to 6
- passage_inner: bfloat16 [1024, 128, 3072], P(('dp', 'group')), may hold values from -6 to 6
- passage_resid: bfloat16 [1024, 128, 768], P(('dp', 'group')), may hold values from -6 to 6
- out_weight: bfloat16 [3072, 768], replicated, may hold values from -0.109375 to 0.109375
- norm_gain: float32 [768], replicated, may hold values from 0.5 to 1.5
- norm_bias: float32 [768], replicated, may hold values from -3 to 3
- proj_weight: bfloat16 [768, 128], replicated, may hold values from -0.21875 to 0.21875
- negative_owner: int32 [1024, 16], P(('dp', 'group')), may hold values from 0 to 127, all different within a row; in each aligned block of 8 rows (0 to 7, 8 to 15, ...) at most 2 rows name the same one
- negative_index: int32 [1024, 16], P(('dp', 'group')), may hold values from 0 to 7, as said below
Outputs:
- query_loss: float32 [1024], P(('dp', 'group'))
- grad_query_inner: bfloat16 [1024, 32, 3072], P(('dp', 'group'))
- grad_query_resid: bfloat16 [1024, 32, 768], P(('dp', 'group'))
- grad_passage_inner: bfloat16 [1024, 128, 3072], P(('dp', 'group'))
- grad_passage_resid: bfloat16 [1024, 128, 768], P(('dp', 'group'))
- grad_out_weight: float32 [3072, 768], replicated
- grad_proj_weight: float32 [768, 128], replicated
- grad_norm: float32 [2, 768], replicated
The draws below stay inside these ranges and needn't reach their ends.
Inputs may be any that keep to these rules, and one draw needn't show every extreme that they name: `negative_owner`: the 16 negatives of one query lie on 16 different devices. Among the queries of one device, no device is named more than 2 times, and in some device's queries one device is named exactly 2 times. `negative_index`: never equal to the query's own position among its device's 8 queries.
All inputs are finite; a program needn't handle non-finite values.
Results may differ from the reference program's by a relative error of at most 0.015.
Values may be sent and summed in bfloat16 or wider, within the bound.
A program may use at most 192 MiB of HBM per device.

```python
import math
import jax
import jax.numpy as jnp
import numpy as np
from jax import lax

HID = 768
FFW = 3072
DIM = 128
QLEN = 32
PLEN = 128
NEG = 16
Q_DEV = 8
QUERIES = 1024
CAP = 2
DEVICES = 128


def draw_negative_index(key, part):
    key = jax.random.fold_in(key, 7)
    offset = jax.random.randint(key, (QUERIES, NEG), 1, Q_DEV)
    own_position = (jnp.arange(QUERIES, dtype=jnp.int32) % Q_DEV)[:, None]
    return ((own_position + offset) % Q_DEV).astype(jnp.int32)


def level_of(key, shape, cuts, low, high):
    def one(axis_at, parts):
        heights = jax.random.uniform(jax.random.fold_in(jax.random.fold_in(key, 6), axis_at), (parts,), jnp.float32, low / len(cuts), high / len(cuts))
        return jnp.repeat(jnp.exp(heights), shape[axis_at] // parts).reshape((-1,) + (1,) * (len(shape) - axis_at - 1))

    loudness = one(*cuts[0])
    for cut in cuts[1:]:
        loudness = loudness * one(*cut)
    return loudness


def routed_block(stream_key, own, number, rows, number_of, top, bound, skew):
    order = jax.random.permutation(stream_key, number_of)
    packed, ordinary = shares(number_of, rows * top, bound, skew, True), shares(number_of, rows * top, bound, skew, False)
    places = jnp.arange(number_of)

    def named(sizes, rotation):
        used = int((sizes > 0).sum())
        fixed = max(1, used // 4)
        moved = fixed + (places - fixed + rotation * (used - fixed)) % max(1, number_of - fixed)
        return jnp.zeros((number_of,), jnp.int32).at[order[jnp.where(places < fixed, places, moved)]].set(jnp.asarray(sizes, jnp.int32))

    sizes = jnp.where(number % 4 == 0, named(packed, number // 4), named(ordinary, number - number // 4 - 1))
    mixed = jax.random.permutation(jax.random.fold_in(own, 3), number_of)
    giver, receiver = mixed[0:number_of // 2 * 2:2], mixed[1:number_of // 2 * 2:2]
    margin = jnp.minimum(sizes[giver] - 1, bound - sizes[receiver]) // 2
    margin = jnp.where((giver == order[0]) | (receiver == order[0]) | (sizes[receiver] == 0), 0, jnp.maximum(margin, 0))
    moved = jax.random.randint(jax.random.fold_in(own, 4), (number_of // 2,), 0, 1 << 20) % (margin + 1)
    sizes = sizes.at[giver].add(-moved).at[receiver].add(moved)
    labels = jnp.searchsorted(jnp.cumsum(sizes), jnp.arange(rows * top), side="right").astype(jnp.int32)
    listing = labels.reshape(top, rows).T
    listing = listing[jax.random.permutation(jax.random.fold_in(own, 1), rows)]
    rotation = jax.random.randint(jax.random.fold_in(own, 2), (rows, 1), 0, top)
    return jnp.take_along_axis(listing, (jnp.arange(top)[None, :] + rotation) % top, axis=1)


def shares(count, total, most, skew, full):
    weights = [(1 << 20) // math.isqrt(standing ** skew) + 1 for standing in range(1, count + 1)]
    largest = most if full else min(most, max(-(-total // count), total * weights[0] // sum(weights)))
    least = 1 if total - largest >= count - 1 else 0
    counts, surplus = [largest] + [least] * (count - 1), total - largest - least * (count - 1)
    while surplus > 0:
        free = [i for i in range(1, count) if counts[i] < largest] or [i for i in range(1, count) if counts[i] < most]
        whole, left = sum([weights[i] for i in free]), surplus
        for i in free:
            extra = min(most - counts[i], max(1, left * weights[i] // whole), surplus)
            counts[i] = counts[i] + extra
            surplus = surplus - extra
    return np.array(counts)


def gaussian(own_key, dims, scale, most, shards=(), held_as=jnp.bfloat16):
    values = scale * jax.random.normal(own_key, dims, jnp.float32)
    if shards:
        values = values * level_of(own_key, dims, shards, -0.22, 0.18)
    return jnp.clip(values, -most, most).astype(held_as)


def setup_inputs(seed: int = 0) -> dict:
    splits = jax.random.split(jax.random.key(seed), 11)
    query_inner = gaussian(splits[0], (QUERIES, QLEN, FFW), 1.0, 6.0, ((0, 128),))
    query_resid = gaussian(splits[1], (QUERIES, QLEN, HID), 1.0, 6.0, ((0, 128),))
    passage_inner = gaussian(splits[2], (QUERIES, PLEN, FFW), 1.0, 6.0, ((0, 128),))
    passage_resid = gaussian(splits[3], (QUERIES, PLEN, HID), 1.0, 6.0, ((0, 128),))
    out_weight = gaussian(splits[4], (FFW, HID), FFW ** -0.5, 0.109375)
    norm_gain = jnp.clip(1.0 + 0.1 * jax.random.normal(splits[5], (HID,), jnp.float32), 0.5, 1.5)
    norm_bias = gaussian(splits[6], (HID,), 0.5, 3.0, (), jnp.float32)
    proj_weight = gaussian(splits[7], (HID, DIM), HID ** -0.5, 0.21875)
    negative_owner_keys = jax.random.split(jax.random.fold_in(splits[8], 1), QUERIES // Q_DEV)
    negative_owner_turns = jax.random.permutation(jax.random.fold_in(splits[8], 3), QUERIES // Q_DEV)
    negative_owner = jax.vmap(lambda own, number: routed_block(jax.random.fold_in(splits[8], 2), own, number, Q_DEV, DEVICES, NEG, CAP, 2))(negative_owner_keys, negative_owner_turns).reshape((QUERIES, NEG))
    negative_index = draw_negative_index(jax.random.fold_in(splits[10], 71), 0)
    return {"query_inner": query_inner, "query_resid": query_resid, "passage_inner": passage_inner, "passage_resid": passage_resid, "out_weight": out_weight, "norm_gain": norm_gain, "norm_bias": norm_bias, "proj_weight": proj_weight, "negative_owner": negative_owner, "negative_index": negative_index}


pool_temp = 0.05
loss_scale = 1024.0
norm_eps = 1e-05
unit_eps = 1e-06

def encode(hidden_in, resid_in, out_weight, norm_gain, norm_bias, proj_weight):
    summed = jnp.dot(hidden_in, out_weight, preferred_element_type=jnp.float32) + resid_in.astype(jnp.float32)
    center = summed - lax.optimization_barrier(jnp.mean(summed, axis=-1, keepdims=True))
    reciprocal = lax.rsqrt(lax.optimization_barrier(jnp.mean(center * center, axis=-1, keepdims=True)) + norm_eps)
    normed = center * reciprocal
    layer_out = (normed * norm_gain + norm_bias).astype(jnp.bfloat16)
    projected = jnp.dot(layer_out, proj_weight, preferred_element_type=jnp.float32)
    length = jnp.sqrt(lax.optimization_barrier(jnp.sum(projected * projected, axis=-1, keepdims=True)) + unit_eps)
    unit_vec = projected / length
    return ((layer_out, normed, reciprocal, length, unit_vec), unit_vec.astype(jnp.bfloat16))

def encode_back(stored, grad_unit, hidden_in, out_weight, norm_gain, proj_weight):
    layer_out, normed, reciprocal, length, unit_vec = stored
    grad_projected = ((grad_unit - unit_vec * lax.optimization_barrier(jnp.sum(unit_vec * grad_unit, axis=-1, keepdims=True))) / length).astype(jnp.bfloat16)
    weight_proj = jnp.dot(layer_out.T, grad_projected, preferred_element_type=jnp.float32)
    grad_layer = jnp.dot(grad_projected, proj_weight.T, preferred_element_type=jnp.float32)
    norm_grads = jnp.stack([lax.optimization_barrier(jnp.sum(grad_layer * normed, axis=0)), lax.optimization_barrier(jnp.sum(grad_layer, axis=0))])
    grad_normed = grad_layer * norm_gain
    grad_summed = (reciprocal * (grad_normed - lax.optimization_barrier(jnp.mean(grad_normed, axis=-1, keepdims=True)) - normed * lax.optimization_barrier(jnp.mean(grad_normed * normed, axis=-1, keepdims=True)))).astype(jnp.bfloat16)
    weight_out = jnp.dot(hidden_in.T, grad_summed, preferred_element_type=jnp.float32)
    grad_hidden = jnp.dot(grad_summed, out_weight.T, preferred_element_type=jnp.float32).astype(jnp.bfloat16)
    return (grad_hidden, grad_summed, weight_out, weight_proj, norm_grads)

def reference(query_inner, query_resid, passage_inner, passage_resid, out_weight, norm_gain, norm_bias, proj_weight, negative_owner, negative_index):
    query_flat = query_inner.reshape(QUERIES * QLEN, FFW)
    passage_flat = passage_inner.reshape(QUERIES * PLEN, FFW)
    query_stored, query_emb = encode(query_flat, query_resid.reshape(QUERIES * QLEN, HID), out_weight, norm_gain, norm_bias, proj_weight)
    passage_stored, passage_emb = encode(passage_flat, passage_resid.reshape(QUERIES * PLEN, HID), out_weight, norm_gain, norm_bias, proj_weight)
    query_wide = query_emb.reshape(QUERIES, QLEN, DIM).astype(jnp.float32)
    passage_emb = passage_emb.reshape(QUERIES, PLEN, DIM)
    negatives = (negative_owner * Q_DEV + negative_index).astype(jnp.int32)
    candidates = jnp.concatenate([jnp.arange(QUERIES, dtype=jnp.int32)[:, None], negatives], axis=1)
    candidate_emb = passage_emb[candidates].astype(jnp.float32)
    logits = jnp.einsum('qid,qcjd->qcij', query_wide, candidate_emb, precision=lax.Precision.HIGHEST) / pool_temp
    exp_logits = jnp.exp(logits)
    totals = lax.optimization_barrier(jnp.sum(exp_logits, axis=-1, keepdims=True))
    pair_score = pool_temp * lax.optimization_barrier(jnp.sum(jnp.log(totals[..., 0]), axis=-1))
    weights = (exp_logits / totals).astype(jnp.bfloat16).astype(jnp.float32)
    exp_scores = jnp.exp(pair_score)
    score_totals = lax.optimization_barrier(jnp.sum(exp_scores, axis=-1, keepdims=True))
    query_loss = jnp.log(score_totals[:, 0]) - pair_score[:, 0]
    target = (jnp.arange(NEG + 1) == 0).astype(jnp.float32)
    seed_grad = loss_scale * (exp_scores / score_totals - target)
    query_pull = jnp.einsum('qcij,qcjd->qcid', weights, candidate_emb, precision=lax.Precision.HIGHEST)
    query_grad = lax.optimization_barrier(jnp.sum(seed_grad[:, :, None, None] * query_pull, axis=1))
    passage_push = seed_grad[:, :, None, None] * jnp.einsum('qcij,qid->qcjd', weights, query_wide, precision=lax.Precision.HIGHEST)
    passage_grad = jax.ops.segment_sum(passage_push.reshape(QUERIES * (NEG + 1), PLEN, DIM), candidates.reshape(-1), num_segments=QUERIES)
    query_back = encode_back(query_stored, query_grad.reshape(QUERIES * QLEN, DIM), query_flat, out_weight, norm_gain, proj_weight)
    passage_back = encode_back(passage_stored, passage_grad.reshape(QUERIES * PLEN, DIM), passage_flat, out_weight, norm_gain, proj_weight)
    return (query_loss, query_back[0].reshape(QUERIES, QLEN, FFW), query_back[1].reshape(QUERIES, QLEN, HID), passage_back[0].reshape(QUERIES, PLEN, FFW), passage_back[1].reshape(QUERIES, PLEN, HID), query_back[2] + passage_back[2], query_back[3] + passage_back[3], query_back[4] + passage_back[4])
```

```python
import jax
import jax.numpy as jnp
from jax import lax
from jax.experimental import pallas as pl
from jax.experimental.pallas import tpu as pltpu
from jax.sharding import PartitionSpec as P

HID = 768
FFW = 3072
DIM = 128
QLEN = 32
PLEN = 128
NEG = 16
Q_DEV = 8


pool_temp = 0.05
loss_scale = 1024.0
MESH = pl.DeviceIdType.MESH
norm_eps = 1e-05
unit_eps = 1e-06


def encode(hidden_in, resid_in, out_weight, norm_gain, norm_bias, proj_weight):
    summed = jnp.dot(hidden_in, out_weight, preferred_element_type=jnp.float32) + resid_in.astype(
        jnp.float32
    )
    center = summed - jnp.mean(summed, axis=-1, keepdims=True)
    reciprocal = lax.rsqrt(jnp.mean(center * center, axis=-1, keepdims=True) + norm_eps)
    normed = center * reciprocal
    layer_out = (normed * norm_gain + norm_bias).astype(jnp.bfloat16)
    projected = jnp.dot(layer_out, proj_weight, preferred_element_type=jnp.float32)
    length = jnp.sqrt(jnp.sum(projected * projected, axis=-1, keepdims=True) + unit_eps)
    unit_vec = projected / length
    return ((layer_out, normed, reciprocal, length, unit_vec), unit_vec.astype(jnp.bfloat16))


def encode_back(stored, grad_unit, hidden_in, out_weight, norm_gain, proj_weight):
    layer_out, normed, reciprocal, length, unit_vec = stored
    grad_projected = (
        (grad_unit - unit_vec * jnp.sum(unit_vec * grad_unit, axis=-1, keepdims=True)) / length
    ).astype(jnp.bfloat16)
    weight_proj = jnp.dot(layer_out.T, grad_projected, preferred_element_type=jnp.float32)
    grad_layer = jnp.dot(grad_projected, proj_weight.T, preferred_element_type=jnp.float32)
    norm_grads = jnp.stack([jnp.sum(grad_layer * normed, axis=0), jnp.sum(grad_layer, axis=0)])
    grad_normed = grad_layer * norm_gain
    grad_summed = (
        reciprocal
        * (
            grad_normed
            - jnp.mean(grad_normed, axis=-1, keepdims=True)
            - normed * jnp.mean(grad_normed * normed, axis=-1, keepdims=True)
        )
    ).astype(jnp.bfloat16)
    weight_out = jnp.dot(hidden_in.T, grad_summed, preferred_element_type=jnp.float32)
    grad_hidden = jnp.dot(grad_summed, out_weight.T, preferred_element_type=jnp.float32).astype(
        jnp.bfloat16
    )
    return (grad_hidden, grad_summed, weight_out, weight_proj, norm_grads)


def pool_scores(query_side, passage_side):
    logits = (
        jnp.einsum(
            "...id,...jd->...ij", query_side, passage_side, preferred_element_type=jnp.float32
        )
        / pool_temp
    )
    exp_logits = jnp.exp(logits)
    totals = jnp.sum(exp_logits, axis=-1, keepdims=True)
    pair_score = pool_temp * jnp.sum(jnp.log(totals[..., 0]), axis=-1)
    return (pair_score, (exp_logits / totals).astype(jnp.bfloat16))


def pull_toward(weights, passage_side):
    return jnp.einsum(
        "...ij,...jd->...id", weights, passage_side, preferred_element_type=jnp.float32
    )


def push_toward(weights, query_side):
    return jnp.einsum("...ij,...id->...jd", weights, query_side, preferred_element_type=jnp.float32)


def softmax_loss(scores):
    exp_scores = jnp.exp(scores)
    totals = jnp.sum(exp_scores, axis=-1, keepdims=True)
    query_loss = jnp.log(totals[:, 0]) - scores[:, 0]
    target = (jnp.arange(scores.shape[-1]) == 0).astype(jnp.float32)
    return (query_loss, loss_scale * (exp_scores / totals - target))


AXES = ("x", "y", "z")
ORDERS = (("x", "y", "z"), ("y", "z", "x"), ("z", "x", "y"), ("x", "y", "z"))
PARTS = 3
PART_ROWS = 3072
SIDE_ROWS = 512


def position():
    dp = lax.axis_index("dp")
    return {"x": dp // 8, "y": lax.axis_index("group"), "z": (dp // 2) % 4, "core": dp % 2}


def device_at(place):
    return ((place["x"] * 4 + place["z"]) * 2 + place["core"], place["y"])


def shifted(place, axis, step):
    return {**place, axis: (place[axis] + step) % (2 if axis == "core" else 4)}


def greet(place):
    barrier = pltpu.get_barrier_semaphore()
    peers = [shifted(place, axis, t) for axis in AXES for t in (1, 2, 3)] + [shifted(place, "core", 1)]
    for peer in peers:
        pl.semaphore_signal(barrier, inc=1, device_id=device_at(peer), device_id_type=MESH)
    pl.semaphore_wait(barrier, len(peers))


def add_rows(out, out_at, terms, rows, chunk):
    def body(i, carry):
        at = pl.multiple_of(i * chunk, chunk)
        total = None
        for ref, start in terms:
            value = ref[pl.ds(pl.multiple_of(start + at, 8), chunk), :].astype(jnp.float32)
            total = value if total is None else total + value
        out[pl.ds(pl.multiple_of(out_at + at, 8), chunk), :] = total.astype(out.dtype)
        return carry

    lax.fori_loop(0, rows // chunk, body, 0)


def sum_kernel(
    grad_ref, side_ref, out_ref, side_out,
    core_in, held, in1, held1, in2, held2, in3,
    score_in, sheld, sin1, sheld1, sin2, sheld2, sin3,
    send_sem, recv_sem,
):
    place = position()
    core = place["core"]
    greet(place)
    copies = {}

    def send(phase, part, step, src, dst, peer):
        copy = pltpu.make_async_remote_copy(
            src_ref=src, dst_ref=dst,
            send_sem=send_sem.at[phase, part, step], recv_sem=recv_sem.at[phase, part, step],
            device_id=device_at(peer), device_id_type=MESH,
        )
        copy.start()
        copies[phase, part, step] = copy

    def bufs(part):
        if part < PARTS:
            return dict(
                src=grad_ref.at[part], core_in=core_in.at[part], held=held.at[part],
                ins=(in1.at[part], in2.at[part], in3.at[part]),
                helds=(held1.at[part], held2.at[part]), out=out_ref.at[part], rows=PART_ROWS,
            )
        return dict(
            src=side_ref, core_in=score_in, held=sheld, ins=(sin1, sin2, sin3),
            helds=(sheld1, sheld2), out=side_out, rows=SIDE_ROWS,
        )

    every = range(PARTS + 1)
    other = (core + 1) % 2
    for part in every:
        b = bufs(part)
        send(0, part, 0, b["src"].at[other], b["core_in"], shifted(place, "core", 1))
    for part in every:
        b = bufs(part)
        copies[0, part, 0].wait_recv()
        add_rows(b["held"], 0, [(b["src"].at[core], 0), (b["core_in"], 0)], b["rows"], 128)
        rows = b["rows"] // 4
        axis = ORDERS[part][0]
        for t in (1, 2, 3):
            peer = shifted(place, axis, t)
            at = pl.multiple_of(peer[axis] * rows, rows)
            send(1, part, t - 1, b["held"].at[pl.ds(at, rows)], b["ins"][0].at[t - 1], peer)
    for phase in (1, 2, 3):
        for part in every:
            b = bufs(part)
            rows = b["rows"] // 4**phase
            axis = ORDERS[part][phase - 1]
            here = b["held"] if phase == 1 else b["helds"][phase - 2]
            for t in (1, 2, 3):
                copies[phase, part, t - 1].wait_recv()
            terms = [(here, place[axis] * rows)] + [(b["ins"][phase - 1].at[t], 0) for t in range(3)]
            if phase < 3:
                target, at = b["helds"][phase - 1], 0
            else:
                target = b["out"].at[core]
                at = sum(place[a] * (b["rows"] // 4 ** (n + 1)) for n, a in enumerate(ORDERS[part]))
            add_rows(target, at, terms, rows, 96 if rows % 96 == 0 else min(rows, 64))
            if phase < 3:
                axis = ORDERS[part][phase]
                rows = rows // 4
                for t in (1, 2, 3):
                    peer = shifted(place, axis, t)
                    start = pl.multiple_of(peer[axis] * rows, rows)
                    send(phase + 1, part, t - 1, target.at[pl.ds(start, rows)], b["ins"][phase].at[t - 1], peer)
            else:
                axis = ORDERS[part][2]
                block = target.at[pl.ds(pl.multiple_of(at, 8 if part == PARTS else 16), rows)]
                for t in (1, 2, 3):
                    send(4, part, t - 1, block, block, shifted(place, axis, t))
    for phase in (4, 5, 6):
        for part in every:
            b = bufs(part)
            for t in (1, 2, 3):
                copies[phase, part, t - 1].wait_recv()
            target = b["out"].at[core]
            if phase < 6:
                depth = 6 - phase
                rows = b["rows"] // 4**depth
                axis = ORDERS[part][depth - 1]
                at = sum(
                    place[a] * (b["rows"] // 4 ** (n + 1)) for n, a in enumerate(ORDERS[part][:depth])
                )
                block = target.at[pl.ds(pl.multiple_of(at, 8 if part == PARTS else 16), rows)]
                for t in (1, 2, 3):
                    send(phase + 1, part, t - 1, block, block, shifted(place, axis, t))
            else:
                send(7, part, 0, target, target, shifted(place, "core", 1))
    for part in every:
        copies[7, part, 0].wait_recv()
    for copy in copies.values():
        copy.wait_send()


def sum_over_devices(grad, side):
    bf, f32 = jnp.bfloat16, jnp.float32
    vm = lambda *shape: pltpu.VMEM(shape, bf)
    vf = lambda *shape: pltpu.VMEM(shape, f32)
    r = PART_ROWS
    s = SIDE_ROWS
    return pl.pallas_call(
        sum_kernel,
        out_shape=(
            jax.ShapeDtypeStruct((PARTS, 2, r, DIM), bf),
            jax.ShapeDtypeStruct((2, s, DIM), f32),
        ),
        in_specs=[pl.BlockSpec(memory_space=pltpu.VMEM)] * 2,
        out_specs=(pl.BlockSpec(memory_space=pltpu.VMEM),) * 2,
        scratch_shapes=[
            vm(PARTS, r, DIM), vm(PARTS, r, DIM), vm(PARTS, 3, r // 4, DIM), vm(PARTS, r // 4, DIM),
            vm(PARTS, 3, r // 16, DIM), vm(PARTS, r // 16, DIM), vm(PARTS, 3, r // 64, DIM),
            vf(s, DIM), vf(s, DIM), vf(3, s // 4, DIM), vf(s // 4, DIM),
            vf(3, s // 16, DIM), vf(s // 16, DIM), vf(3, s // 64, DIM),
            pltpu.SemaphoreType.DMA((8, PARTS + 1, 3)),
            pltpu.SemaphoreType.DMA((8, PARTS + 1, 3)),
        ],
        compiler_params=pltpu.CompilerParams(
            collective_id=3, has_side_effects=True, vmem_limit_bytes=48 * 1024 * 1024
        ),
        name="grad_sum",
    )(grad, side)


def summed_grads(weight_out, weight_proj, norm_grads):
    grad = (
        weight_out.astype(jnp.bfloat16)
        .reshape(2, FFW // 2, PARTS, 2, DIM)
        .transpose(2, 0, 3, 1, 4)
        .reshape(PARTS, 2, PART_ROWS, DIM)
    )
    side = jnp.concatenate(
        [weight_proj, norm_grads.reshape(2 * HID // DIM, DIM),
         jnp.zeros((2 * SIDE_ROWS - HID - 2 * HID // DIM, DIM), jnp.float32)]
    ).reshape(2, SIDE_ROWS, DIM)
    grad, side = sum_over_devices(grad, side)
    total = (
        grad.reshape(PARTS, 2, 2, FFW // 2, DIM)
        .transpose(1, 3, 0, 2, 4)
        .reshape(FFW, HID)
        .astype(jnp.float32)
    )
    side = side.reshape(2 * SIDE_ROWS, DIM)
    return total, side[:HID], side[HID : HID + 2 * HID // DIM].reshape(2, HID)


def local(
    query_inner,
    query_resid,
    passage_inner,
    passage_resid,
    out_weight,
    norm_gain,
    norm_bias,
    proj_weight,
    negative_owner,
    negative_index,
):
    devices = lax.axis_size(("dp", "group"))
    capacity = max(2, 2 * Q_DEV * NEG // devices)
    slot_total = devices * capacity
    query_flat = query_inner.reshape(Q_DEV * QLEN, FFW)
    passage_flat = passage_inner.reshape(Q_DEV * PLEN, FFW)
    query_stored, query_emb = encode(
        query_flat,
        query_resid.reshape(Q_DEV * QLEN, HID),
        out_weight,
        norm_gain,
        norm_bias,
        proj_weight,
    )
    passage_stored, passage_emb = encode(
        passage_flat,
        passage_resid.reshape(Q_DEV * PLEN, HID),
        out_weight,
        norm_gain,
        norm_bias,
        proj_weight,
    )
    query_emb = query_emb.reshape(Q_DEV, QLEN, DIM)
    passage_emb = passage_emb.reshape(Q_DEV, PLEN, DIM)
    pair_owner = negative_owner.reshape(-1)
    owner_hot = (pair_owner[:, None] == jnp.arange(devices, dtype=jnp.int32)[None, :]).astype(
        jnp.int32
    )
    pair_rank = jnp.sum((jnp.cumsum(owner_hot, axis=0) - owner_hot) * owner_hot, axis=1)
    pair_slot = pair_owner * capacity + pair_rank
    wanted = jnp.full((slot_total,), Q_DEV, jnp.int32).at[pair_slot].set(negative_index.reshape(-1))
    requested = lax.all_to_all(wanted, ("dp", "group"), split_axis=0, concat_axis=0, tiled=True)
    served = jnp.minimum(requested, Q_DEV - 1)
    gather_hot = (
        (served[None, :] == jnp.arange(Q_DEV, dtype=jnp.int32)[:, None])
        & (requested[None, :] < Q_DEV)
    ).astype(jnp.float32)
    anchor_score, anchor_weights = pool_scores(query_emb, passage_emb)
    anchor_pull = pull_toward(anchor_weights, passage_emb)
    anchor_push = push_toward(anchor_weights, query_emb)
    fetched = lax.all_to_all(
        passage_emb[served], ("dp", "group"), split_axis=0, concat_axis=0, tiled=True
    )
    negative_rows = fetched[pair_slot].reshape(Q_DEV, NEG, PLEN, DIM)
    query_wide = jnp.broadcast_to(query_emb[:, None], (Q_DEV, NEG, QLEN, DIM))
    negative_score, negative_weights = pool_scores(query_wide, negative_rows)
    query_loss, seed_grad = softmax_loss(
        jnp.concatenate([anchor_score[:, None], negative_score], axis=1)
    )
    negative_seed = seed_grad[:, 1:, None, None]
    negative_pull = negative_seed * pull_toward(negative_weights, negative_rows)
    negative_push = negative_seed * push_toward(negative_weights, query_wide)
    outgoing = (
        jnp.zeros((slot_total, PLEN, DIM), jnp.float32)
        .at[pair_slot]
        .set(negative_push.reshape(Q_DEV * NEG, PLEN, DIM))
    )
    returned = lax.all_to_all(
        outgoing.astype(jnp.bfloat16), ("dp", "group"), split_axis=0, concat_axis=0, tiled=True
    ).astype(outgoing.dtype)
    query_grad = seed_grad[:, 0, None, None] * anchor_pull + jnp.sum(negative_pull, axis=1)
    remote_push = jnp.dot(
        gather_hot, returned.reshape(slot_total, PLEN * DIM), precision=lax.Precision.HIGHEST
    )
    passage_grad = seed_grad[:, 0, None, None] * anchor_push + remote_push.reshape(Q_DEV, PLEN, DIM)
    query_back = encode_back(
        query_stored,
        query_grad.reshape(Q_DEV * QLEN, DIM),
        query_flat,
        out_weight,
        norm_gain,
        proj_weight,
    )
    passage_back = encode_back(
        passage_stored,
        passage_grad.reshape(Q_DEV * PLEN, DIM),
        passage_flat,
        out_weight,
        norm_gain,
        proj_weight,
    )
    summed = summed_grads(
        query_back[2] + passage_back[2],
        query_back[3] + passage_back[3],
        query_back[4] + passage_back[4],
    )
    return (
        query_loss,
        query_back[0].reshape(Q_DEV, QLEN, FFW),
        query_back[1].reshape(Q_DEV, QLEN, HID),
        passage_back[0].reshape(Q_DEV, PLEN, FFW),
        passage_back[1].reshape(Q_DEV, PLEN, HID),
        summed[0],
        summed[1],
        summed[2],
    )


def solution(mesh):
    in_specs = (
        P(("dp", "group"), None, None),
        P(("dp", "group"), None, None),
        P(("dp", "group"), None, None),
        P(("dp", "group"), None, None),
        P(),
        P(),
        P(),
        P(),
        P(("dp", "group"), None),
        P(("dp", "group"), None),
    )
    out_specs = (
        P(("dp", "group")),
        P(("dp", "group"), None, None),
        P(("dp", "group"), None, None),
        P(("dp", "group"), None, None),
        P(("dp", "group"), None, None),
        P(),
        P(),
        P(),
    )
    return jax.shard_map(local, mesh=mesh, in_specs=in_specs, out_specs=out_specs, check_vma=False)
```

```python
import functools

import jax
import jax.numpy as jnp
from jax import lax
from jax.experimental import pallas as pl
from jax.experimental.pallas import tpu as pltpu
from jax.sharding import PartitionSpec as P

HID = 768
FFW = 3072
DIM = 128
QLEN = 32
PLEN = 128
NEG = 16
Q_DEV = 8
DEVICES = 128
CAP = 2
Q_ROWS = Q_DEV * QLEN
P_ROWS = Q_DEV * PLEN
ROWS = Q_ROWS + P_ROWS
CHUNK = 256
SLOTS = DEVICES * CAP
BLOCKS = SLOTS // 8 + Q_DEV
SORTED = BLOCKS * 8
WIDE = 384

MESH = pl.DeviceIdType.MESH
MIB = 1024 * 1024
bf16 = jnp.bfloat16
f32 = jnp.float32

pool_temp = 0.05
loss_scale = 1024.0
norm_eps = 1e-05
unit_eps = 1e-06

AXES = ("x", "y", "z")
ORDERS = (("x", "y", "z"), ("y", "z", "x"), ("z", "x", "y"), ("x", "y", "z"))
PARTS = 3
PART_ROWS = 3072
SIDE_ROWS = 512


def position():
    dp = lax.axis_index("dp")
    return {"x": dp // 8, "y": lax.axis_index("group"), "z": (dp // 2) % 4, "core": dp % 2}


def device_at(place):
    return ((place["x"] * 4 + place["z"]) * 2 + place["core"], place["y"])


def number_of(place):
    return place["x"] * 32 + place["z"] * 8 + place["core"] * 4 + place["y"]


def shifted(place, axis, step):
    return {**place, axis: (place[axis] + step) % (2 if axis == "core" else 4)}


def offset(place, t, sign):
    return {
        "x": (place["x"] + sign * (t // 32) + 4) % 4,
        "z": (place["z"] + sign * ((t // 8) % 4) + 4) % 4,
        "core": (place["core"] + sign * ((t // 4) % 2) + 2) % 2,
        "y": (place["y"] + sign * (t % 4) + 4) % 4,
    }


def dot(a, b, contract):
    return lax.dot_general(a, b, ((contract[:1], contract[1:]), ((), ())), preferred_element_type=f32)


def iota(shape, axis):
    return lax.broadcasted_iota(jnp.int32, shape, axis)


def count_of(mask, axis):
    return jnp.sum(jnp.where(mask, 1, 0), axis=axis, keepdims=True)


def pair_table(codes):
    passage = codes % 16
    sub = iota((SLOTS, 1), 0)
    slot = 2 * (sub % DEVICES) + sub // DEVICES
    square0, square1 = iota((SLOTS, SLOTS), 0), iota((SLOTS, SLOTS), 1)
    passage_row = jnp.sum(jnp.where(square0 == square1, passage, 0), axis=0, keepdims=True)
    rank = count_of((passage_row == passage) & (square1 < square0), 1)
    lane = iota((1, DIM), 1)
    blocks = jnp.where(lane < Q_DEV, (count_of(passage == lane, 0) + 7) // 8, 0)
    start = jnp.sum(jnp.where(lane < passage, blocks, 0), axis=1, keepdims=True)
    place = jnp.where(passage < Q_DEV, start * 8 + rank, SORTED)
    wide = iota((1, WIDE), 1)
    hit = (place == wide) & (wide < SORTED)
    order = jnp.sum(jnp.where(hit, slot - SLOTS, 0), axis=0, keepdims=True) + SLOTS
    order_sub = jnp.sum(jnp.where(hit, sub - SLOTS, 0), axis=0, keepdims=True) + SLOTS
    place_row = jnp.sum(jnp.where(slot == wide, place, 0), axis=0, keepdims=True)
    owner = jnp.zeros((1, WIDE), jnp.int32)
    goes_on = jnp.ones((1, WIDE), jnp.int32)
    last = jnp.zeros((1, WIDE), jnp.int32)
    for p in range(Q_DEV):
        begin = jnp.sum(jnp.where(lane < p, blocks, 0), axis=1, keepdims=True)
        end = jnp.sum(jnp.where(lane <= p, blocks, 0), axis=1, keepdims=True)
        owner += jnp.where(wide >= end, 1, 0)
        goes_on -= jnp.where((wide == begin) & (end > begin), 1, 0)
        last += jnp.where(wide == p, jnp.where(end > begin, end - 1, BLOCKS), 0)
    owner = jnp.minimum(owner, Q_DEV - 1)
    return jnp.concatenate([order, order_sub, place_row, owner, goes_on, last, last, last], axis=0)


def pool(query_side, passage_side):
    exp_logits = jnp.exp(dot(query_side, passage_side, (1, 1)) * (1.0 / pool_temp))
    totals = jnp.sum(exp_logits, axis=1, keepdims=True)
    weights = (exp_logits / totals).astype(bf16)
    queries = query_side.shape[0] // QLEN
    logs = jnp.broadcast_to(jnp.log(totals), (queries * QLEN, DIM)).reshape(queries, QLEN, DIM)
    return weights, pool_temp * jnp.sum(logs, axis=1)


def pair_kernel(
    slot_query, slot_of, codes,
    query_inner, query_resid, passage_inner, passage_resid, out_weight, gain, bias, proj,
    normed_out, unit_out, scale_out, grad_out, loss_out,
    inner, resid, weight, query_emb, passage_emb, codes_in, table, table_s,
    asks_out, asks_in, sorted_q, sorted_w, sorted_pull, sorted_exp, slot_exp, slot_seed, block_seed, chain,
    pulls_out, pulls_in, anchor_w, anchor_pull, anchor_score,
    sums, sums_in1, sums_in2,
    load_sem, table_sem, code_send, code_recv, ask_send, ask_recv, pull_send, pull_recv, sum_send, sum_recv,
):
    place = position()
    me = number_of(place)
    lane_row = iota((1, DIM), 1)

    loads = [
        pltpu.make_async_copy(out_weight, weight, load_sem.at[0]),
        pltpu.make_async_copy(query_inner, inner.at[pl.ds(0, Q_ROWS)], load_sem.at[1]),
        pltpu.make_async_copy(query_resid, resid.at[pl.ds(0, Q_ROWS)], load_sem.at[2]),
        pltpu.make_async_copy(passage_inner, inner.at[pl.ds(Q_ROWS, P_ROWS)], load_sem.at[3]),
        pltpu.make_async_copy(passage_resid, resid.at[pl.ds(Q_ROWS, P_ROWS)], load_sem.at[4]),
    ]
    for load in loads:
        load.start()

    barrier = pltpu.get_barrier_semaphore()

    def greet(t, carry):
        pl.semaphore_signal(barrier, inc=1, device_id=device_at(offset(place, t, 1)), device_id_type=MESH)
        return carry

    lax.fori_loop(1, DEVICES, greet, 0)
    asks_in[SLOTS] = jnp.zeros((QLEN, DIM), bf16)
    sorted_pull[SORTED] = jnp.zeros((QLEN, DIM), bf16)
    sorted_exp[SORTED] = jnp.zeros((1, DIM), f32)
    slot_seed[SLOTS] = jnp.zeros((1, DIM), f32)
    chain[BLOCKS] = jnp.zeros((PLEN, DIM), f32)
    codes_in[0] = codes[0]
    pl.semaphore_wait(barrier, DEVICES - 1)

    def code_copy(t):
        return pltpu.make_async_remote_copy(
            src_ref=codes.at[t], dst_ref=codes_in.at[t], send_sem=code_send, recv_sem=code_recv,
            device_id=device_at(offset(place, t, 1)), device_id_type=MESH,
        )

    def send_code(t, carry):
        code_copy(t).start()
        return carry

    lax.fori_loop(1, DEVICES, send_code, 0)

    def encode(at):
        at = pl.multiple_of(at, CHUNK)
        here = pl.ds(at, CHUNK)
        summed = dot(inner[here, :], weight[...], (1, 0)) + resid[here, :].astype(f32)
        center = summed - jnp.mean(summed, axis=1, keepdims=True)
        reciprocal = lax.rsqrt(jnp.mean(center * center, axis=1, keepdims=True) + norm_eps)
        normed = center * reciprocal
        normed_out[here, :] = normed
        layer_out = (normed * gain[...] + bias[...]).astype(bf16)
        projected = dot(layer_out, proj[...], (1, 0))
        length = jnp.sqrt(jnp.sum(projected * projected, axis=1, keepdims=True) + unit_eps)
        unit = projected / length
        unit_out[here, :] = unit
        scale_out[here, :] = jnp.where(iota((CHUNK, DIM), 1) < DIM // 2, reciprocal, length)
        return unit.astype(bf16)

    for load in loads[:3]:
        load.wait()
    query_emb[...] = encode(0).reshape(Q_DEV, QLEN, DIM)

    def ask_copy(t):
        rows = pl.ds(t * CAP, CAP)
        return pltpu.make_async_remote_copy(
            src_ref=asks_out.at[rows], dst_ref=asks_in.at[rows], send_sem=ask_send, recv_sem=ask_recv,
            device_id=device_at(offset(place, t, 1)), device_id_type=MESH,
        )

    def take_query(s):
        return query_emb[slot_query[s]]

    for r in range(CAP):
        asks_in[r] = take_query(r)

    def send_ask(t, carry):
        for r in range(CAP):
            asks_out[t * CAP + r] = take_query(t * CAP + r)
        ask_copy(t).start()
        return carry

    lax.fori_loop(1, DEVICES, send_ask, 0)

    for load in loads[3:]:
        load.wait()

    def encode_passages(i, carry):
        passages = encode((i + 1) * CHUNK).reshape(CHUNK // PLEN, PLEN, DIM)
        passage_emb[pl.ds(i * (CHUNK // PLEN), CHUNK // PLEN)] = passages
        return carry

    lax.fori_loop(0, P_ROWS // CHUNK, encode_passages, 0)

    rest = pl.ds(1, DEVICES - 1)
    everyone = pltpu.make_async_remote_copy(
        src_ref=codes.at[rest], dst_ref=codes_in.at[rest], send_sem=code_send, recv_sem=code_recv,
        device_id=device_at(offset(place, 1, 1)), device_id_type=MESH,
    )
    everyone.wait()
    code_rows = codes_in[...].reshape(DEVICES, DIM)
    slot_codes = jnp.concatenate([code_rows[:, r : r + 1] for r in range(CAP)], axis=0)
    table[...] = pair_table(slot_codes)
    to_scalar = pltpu.make_async_copy(table, table_s, table_sem)
    to_scalar.start()

    def anchor(i, carry):
        rows = pl.ds(pl.multiple_of(i * QLEN, QLEN), QLEN)
        passage = passage_emb[i]
        weights, score = pool(query_emb[i], passage)
        anchor_w[rows, :] = weights
        anchor_pull[rows, :] = dot(weights, passage, (1, 0))
        anchor_score[pl.ds(i, 1), :] = score
        return carry

    lax.fori_loop(0, Q_DEV, anchor, 0)
    to_scalar.wait()

    def asked(buffer):
        return buffer.at[pl.ds(CAP, (DEVICES - 1) * CAP)]

    all_asks = pltpu.make_async_remote_copy(
        src_ref=asked(asks_out), dst_ref=asked(asks_in), send_sem=ask_send, recv_sem=ask_recv,
        device_id=device_at(offset(place, 1, 1)), device_id_type=MESH,
    )
    all_asks.wait()

    def score_block(b, carry):
        at = pl.multiple_of(b * CHUNK, CHUNK)
        for k in range(8):
            asking = asks_in[table_s[0, b * 8 + k]]
            sorted_q[pl.ds(pl.multiple_of(at + k * QLEN, QLEN), QLEN), :] = asking
        passage = passage_emb[table_s[3, b]]
        weights, score = pool(sorted_q[pl.ds(at, CHUNK), :], passage)
        sorted_w[pl.ds(at, CHUNK), :] = weights
        exp_score = jnp.exp(score)
        sorted_exp[pl.ds(b * 8, 8)] = exp_score.reshape(8, 1, DIM)
        pull = dot(weights, passage, (1, 0)).reshape(8, QLEN, DIM) * exp_score.reshape(8, 1, DIM)
        sorted_pull[pl.ds(b * 8, 8)] = pull.astype(bf16)
        return carry

    lax.fori_loop(0, BLOCKS, score_block, 0)

    def exp_of(t, carry):
        for r in range(CAP):
            slot_exp[pl.ds(r * DEVICES + t, 1), :] = sorted_exp[table_s[2, t * CAP + r]]
        return carry

    lax.fori_loop(0, DEVICES, exp_of, 0)

    t_col = iota((DEVICES, 1), 0)
    source = (
        ((place["x"] + 4 - t_col // 32) % 4) * 32
        + ((place["z"] + 4 - (t_col // 8) % 4) % 4) * 8
        + ((place["core"] + 2 - (t_col // 4) % 2) % 2) * 4
        + (place["y"] + 4 - t_col % 4) % 4
    )
    from_device = source == iota((DEVICES, DEVICES), 1)
    query_index = [(slot_codes[r * DEVICES : (r + 1) * DEVICES] // 16).astype(f32) for r in range(CAP)]
    eight = iota((Q_DEV, DIM), 0).astype(f32)
    own_exp = jnp.exp(anchor_score[...])
    spread = jnp.where(iota((Q_DEV, DIM), 1) == me, own_exp, 0.0)
    for r in range(CAP):
        exps = slot_exp[pl.ds(r * DEVICES, DEVICES), :]
        exp_row = jnp.sum(jnp.where(from_device, exps, 0.0), axis=0, keepdims=True)
        index_row = jnp.sum(jnp.where(from_device, query_index[r], 0.0), axis=0, keepdims=True)
        spread += jnp.where(eight == index_row, exp_row, 0.0)
    sums[0] = spread
    near, far = [], []
    for t in range(1, 8):
        peer = shifted(shifted(place, "core", t // 4), "y", t % 4)
        near.append(pltpu.make_async_remote_copy(
            src_ref=sums.at[0], dst_ref=sums_in1.at[t - 1], send_sem=sum_send.at[t - 1],
            recv_sem=sum_recv.at[t - 1], device_id=device_at(peer), device_id_type=MESH,
        ))
    for t in range(1, 16):
        peer = shifted(shifted(place, "x", t // 4), "z", t % 4)
        far.append(pltpu.make_async_remote_copy(
            src_ref=sums.at[1], dst_ref=sums_in2.at[t - 1], send_sem=sum_send.at[t + 6],
            recv_sem=sum_recv.at[t + 6], device_id=device_at(peer), device_id_type=MESH,
        ))
    for copy in near:
        copy.start()

    def pull_copy(t):
        rows = pl.ds(t * CAP, CAP)
        return pltpu.make_async_remote_copy(
            src_ref=pulls_out.at[rows], dst_ref=pulls_in.at[rows], send_sem=pull_send, recv_sem=pull_recv,
            device_id=device_at(offset(place, t, -1)), device_id_type=MESH,
        )

    def take_pull(s):
        return sorted_pull[table_s[2, s]]

    for copy in near:
        copy.wait_recv()
    sums[1] = sums[0] + jnp.sum(sums_in1[...], axis=0)
    for copy in far:
        copy.start()

    for r in range(CAP):
        pulls_in[r] = take_pull(r)

    def send_pull(t, carry):
        for r in range(CAP):
            pulls_out[t * CAP + r] = take_pull(t * CAP + r)
        pull_copy(t).start()
        return carry

    lax.fori_loop(1, DEVICES, send_pull, 0)
    for copy in far:
        copy.wait_recv()
    total = sums[1] + jnp.sum(sums_in2[...], axis=0)

    for r in range(CAP):
        mine = jnp.zeros((DEVICES, DIM), f32)
        for i in range(Q_DEV):
            mine += jnp.where(from_device & (query_index[r] == float(i)), total[i : i + 1, :], 0.0)
        slot_total = jnp.sum(mine, axis=1, keepdims=True)
        here = pl.ds(r * DEVICES, DEVICES)
        slot_seed[here] = (loss_scale * (slot_exp[here, :] / slot_total)).reshape(DEVICES, 1, DIM)

    def push_block(b, carry):
        at = pl.multiple_of(b * CHUNK, CHUNK)
        for k in range(8):
            block_seed[pl.ds(k, 1), :] = slot_seed[table_s[1, b * 8 + k]]
        seeds = block_seed[...].reshape(8, 1, DIM)
        weights = sorted_w[pl.ds(at, CHUNK), :].astype(f32).reshape(8, QLEN, DIM) * seeds
        push = dot(weights.reshape(CHUNK, DIM).astype(bf16), sorted_q[pl.ds(at, CHUNK), :], (0, 0))
        goes_on = table_s[4, b].astype(f32)
        carry = carry * goes_on + push
        chain[b] = carry
        return carry

    lax.fori_loop(0, BLOCKS, push_block, jnp.zeros((PLEN, DIM), f32))

    own_total = jnp.sum(jnp.where(iota((Q_DEV, DIM), 1) == me, total, 0.0), axis=1, keepdims=True)
    own_total = jnp.broadcast_to(own_total, (Q_DEV, DIM))
    anchor_seed = loss_scale * (own_exp / own_total - 1.0)
    loss_out[...] = jnp.log(own_total) - anchor_score[...]
    for p in range(Q_DEV):
        push = dot(anchor_w[pl.ds(p * QLEN, QLEN), :], query_emb[p], (0, 0)) * anchor_seed[p : p + 1, :]
        push += chain[table_s[5, p]]
        grad_out[pl.ds(Q_ROWS + p * PLEN, PLEN), :] = push

    pltpu.make_async_remote_copy(
        src_ref=asked(pulls_out), dst_ref=asked(pulls_in), send_sem=pull_send, recv_sem=pull_recv,
        device_id=device_at(offset(place, 1, 1)), device_id_type=MESH,
    ).wait()
    query_scale = loss_scale / own_total
    for i in range(Q_DEV):
        rows = pl.ds(i * QLEN, QLEN)
        pull = jnp.zeros((QLEN, DIM), f32)
        for k in range(NEG):
            pull += pulls_in[slot_of[i * NEG + k]].astype(f32)
        grad_out[rows, :] = (
            pull * query_scale[i : i + 1, :] + anchor_pull[rows, :] * anchor_seed[i : i + 1, :]
        )
    for copy in near + far:
        copy.wait_send()


def pair_grads(slot_query, slot_of, codes, query_inner, query_resid, passage_inner, passage_resid,
               out_weight, gain, bias, proj):
    any_, vmem, smem = pl.ANY, pltpu.VMEM, pltpu.SMEM
    spec = lambda space: pl.BlockSpec(memory_space=space)
    dma = pltpu.SemaphoreType.DMA
    return pl.pallas_call(
        pair_kernel,
        out_shape=(
            jax.ShapeDtypeStruct((ROWS, HID), f32),
            jax.ShapeDtypeStruct((ROWS, DIM), f32),
            jax.ShapeDtypeStruct((ROWS, DIM), f32),
            jax.ShapeDtypeStruct((ROWS, DIM), f32),
            jax.ShapeDtypeStruct((Q_DEV, DIM), f32),
        ),
        in_specs=[spec(smem), spec(smem), spec(vmem)] + [spec(any_)] * 5 + [spec(vmem)] * 3,
        out_specs=(spec(vmem),) * 5,
        scratch_shapes=[
            vmem((ROWS, FFW), bf16),
            vmem((ROWS, HID), bf16),
            vmem((FFW, HID), bf16),
            vmem((Q_DEV, QLEN, DIM), bf16),
            vmem((Q_DEV, PLEN, DIM), bf16),
            vmem((DEVICES, 1, DIM), jnp.int32),
            vmem((8, WIDE), jnp.int32),
            smem((8, WIDE), jnp.int32),
            vmem((SLOTS, QLEN, DIM), bf16),
            vmem((SLOTS + 1, QLEN, DIM), bf16),
            vmem((SORTED * QLEN, DIM), bf16),
            vmem((SORTED * QLEN, DIM), bf16),
            vmem((SORTED + 1, QLEN, DIM), bf16),
            vmem((SORTED + 1, 1, DIM), f32),
            vmem((SLOTS, DIM), f32),
            vmem((SLOTS + 1, 1, DIM), f32),
            vmem((8, DIM), f32),
            vmem((BLOCKS + 1, PLEN, DIM), f32),
            vmem((SLOTS, QLEN, DIM), bf16),
            vmem((SLOTS, QLEN, DIM), bf16),
            vmem((Q_ROWS, DIM), bf16),
            vmem((Q_ROWS, DIM), f32),
            vmem((Q_DEV, DIM), f32),
            vmem((2, Q_DEV, DIM), f32),
            vmem((7, Q_DEV, DIM), f32),
            vmem((15, Q_DEV, DIM), f32),
            dma((5,)), dma, dma, dma, dma, dma, dma, dma, dma((22,)), dma((22,)),
        ],
        compiler_params=pltpu.CompilerParams(
            collective_id=1, has_side_effects=True, vmem_limit_bytes=58 * MIB
        ),
        name="pair_grads",
    )(slot_query, slot_of, codes, query_inner, query_resid, passage_inner, passage_resid, out_weight,
      gain, bias, proj)


def add_rows(out, out_at, terms, rows, chunk):
    def body(i, carry):
        at = pl.multiple_of(i * chunk, chunk)
        total = None
        for ref, start in terms:
            value = ref[pl.ds(pl.multiple_of(start + at, 8), chunk), :].astype(f32)
            total = value if total is None else total + value
        out[pl.ds(pl.multiple_of(out_at + at, 8), chunk), :] = total.astype(out.dtype)
        return carry

    lax.fori_loop(0, rows // chunk, body, 0)


def back_kernel(
    query_inner, passage_inner, normed, unit, scale, grad_unit, gain, bias, proj,
    grad_summed, out_ref, side_out,
    inner, grad, side, proj_sum,
    core_in, held, in1, held1, in2, held2, in3,
    score_in, sheld, sin1, sheld1, sin2, sheld2, sin3,
    load_sem, send_sem, recv_sem,
):
    place = position()
    core = place["core"]
    other = (core + 1) % 2
    loads = [
        pltpu.make_async_copy(query_inner, inner.at[pl.ds(0, Q_ROWS)], load_sem.at[0]),
        pltpu.make_async_copy(passage_inner, inner.at[pl.ds(Q_ROWS, P_ROWS)], load_sem.at[1]),
    ]
    for load in loads:
        load.start()
    barrier = pltpu.get_barrier_semaphore()
    peers = [shifted(place, axis, t) for axis in AXES for t in (1, 2, 3)] + [shifted(place, "core", 1)]
    for peer in peers:
        pl.semaphore_signal(barrier, inc=1, device_id=device_at(peer), device_id_type=MESH)

    proj_sum[...] = jnp.zeros_like(proj_sum)

    def back(i, carry):
        here = pl.ds(pl.multiple_of(i * CHUNK, CHUNK), CHUNK)
        u, g = unit[here, :], grad_unit[here, :]
        reciprocal = scale[here, 0:1]
        length = scale[here, DIM - 1 : DIM]
        grad_projected = ((g - u * jnp.sum(u * g, axis=1, keepdims=True)) / length).astype(bf16)
        n = normed[here, :]
        layer_out = (n * gain[...] + bias[...]).astype(bf16)
        proj_sum[...] += dot(layer_out, grad_projected, (0, 0))
        grad_layer = dot(grad_projected, proj[...], (1, 1))
        norm_sums = (
            carry[0] + jnp.sum(grad_layer * n, axis=0, keepdims=True),
            carry[1] + jnp.sum(grad_layer, axis=0, keepdims=True),
        )
        grad_normed = grad_layer * gain[...]
        grad_summed[here, :] = (
            reciprocal
            * (
                grad_normed
                - jnp.mean(grad_normed, axis=1, keepdims=True)
                - n * jnp.mean(grad_normed * n, axis=1, keepdims=True)
            )
        ).astype(bf16)
        return norm_sums

    zero = jnp.zeros((1, HID), f32)
    norm_sums = lax.fori_loop(0, ROWS // CHUNK, back, (zero, zero))
    side[0] = proj_sum[0:SIDE_ROWS, :]
    side[1] = jnp.zeros((SIDE_ROWS, DIM), f32)
    side[1, 0 : HID - SIDE_ROWS, :] = proj_sum[SIDE_ROWS:HID, :]
    for n in range(2):
        for j in range(HID // DIM):
            row = HID - SIDE_ROWS + n * (HID // DIM) + j
            side[1, row : row + 1, :] = norm_sums[n][:, j * DIM : (j + 1) * DIM]

    copies = {}

    def send(phase, part, step, src, dst, peer):
        copy = pltpu.make_async_remote_copy(
            src_ref=src, dst_ref=dst,
            send_sem=send_sem.at[phase, part, step], recv_sem=recv_sem.at[phase, part, step],
            device_id=device_at(peer), device_id_type=MESH,
        )
        copy.start()
        copies[phase, part, step] = copy

    def bufs(part):
        if part < PARTS:
            return dict(
                src=grad.at[part], core_in=core_in.at[part], held=held.at[part],
                ins=(in1.at[part], in2.at[part], in3.at[part]),
                helds=(held1.at[part], held2.at[part]), out=out_ref.at[part], rows=PART_ROWS,
            )
        return dict(
            src=side, core_in=score_in, held=sheld, ins=(sin1, sin2, sin3),
            helds=(sheld1, sheld2), out=side_out, rows=SIDE_ROWS,
        )

    every = range(PARTS + 1)
    pl.semaphore_wait(barrier, len(peers))
    for load in loads:
        load.wait()

    def weights(half):
        def block(g, carry):
            start = pl.multiple_of(half * (FFW // 2) + g * 512, 512)
            product = dot(inner[:, pl.ds(start, 512)], grad_summed[...], (0, 0)).astype(bf16)
            for part in range(PARTS):
                for h in range(2):
                    column = part * 256 + h * DIM
                    at = pl.multiple_of(h * (FFW // 2) + g * 512, 512)
                    grad[part, half, pl.ds(at, 512), :] = product[:, column : column + DIM]
            return carry

        lax.fori_loop(0, 3, block, 0)

    def send_half(part):
        b = bufs(part)
        send(0, part, 0, b["src"].at[other], b["core_in"], shifted(place, "core", 1))

    send_half(PARTS)
    weights(other)
    for part in range(PARTS):
        send_half(part)
    weights(core)

    for part in every:
        b = bufs(part)
        copies[0, part, 0].wait_recv()
        add_rows(b["held"], 0, [(b["src"].at[core], 0), (b["core_in"], 0)], b["rows"], 128)
        rows = b["rows"] // 4
        axis = ORDERS[part][0]
        for t in (1, 2, 3):
            peer = shifted(place, axis, t)
            at = pl.multiple_of(peer[axis] * rows, rows)
            send(1, part, t - 1, b["held"].at[pl.ds(at, rows)], b["ins"][0].at[t - 1], peer)
    for phase in (1, 2, 3):
        for part in every:
            b = bufs(part)
            rows = b["rows"] // 4**phase
            axis = ORDERS[part][phase - 1]
            here = b["held"] if phase == 1 else b["helds"][phase - 2]
            for t in (1, 2, 3):
                copies[phase, part, t - 1].wait_recv()
            terms = [(here, place[axis] * rows)] + [(b["ins"][phase - 1].at[t], 0) for t in range(3)]
            if phase < 3:
                target, at = b["helds"][phase - 1], 0
            else:
                target = b["out"].at[core]
                at = sum(place[a] * (b["rows"] // 4 ** (n + 1)) for n, a in enumerate(ORDERS[part]))
            add_rows(target, at, terms, rows, 96 if rows % 96 == 0 else min(rows, 64))
            if phase < 3:
                axis = ORDERS[part][phase]
                rows = rows // 4
                for t in (1, 2, 3):
                    peer = shifted(place, axis, t)
                    start = pl.multiple_of(peer[axis] * rows, rows)
                    send(phase + 1, part, t - 1, target.at[pl.ds(start, rows)], b["ins"][phase].at[t - 1], peer)
            else:
                axis = ORDERS[part][2]
                block = target.at[pl.ds(pl.multiple_of(at, 8 if part == PARTS else 16), rows)]
                for t in (1, 2, 3):
                    send(4, part, t - 1, block, block, shifted(place, axis, t))
    for phase in (4, 5, 6):
        for part in every:
            b = bufs(part)
            for t in (1, 2, 3):
                copies[phase, part, t - 1].wait_recv()
            target = b["out"].at[core]
            if phase < 6:
                depth = 6 - phase
                rows = b["rows"] // 4**depth
                axis = ORDERS[part][depth - 1]
                at = sum(
                    place[a] * (b["rows"] // 4 ** (n + 1)) for n, a in enumerate(ORDERS[part][:depth])
                )
                block = target.at[pl.ds(pl.multiple_of(at, 8 if part == PARTS else 16), rows)]
                for t in (1, 2, 3):
                    send(phase + 1, part, t - 1, block, block, shifted(place, axis, t))
            else:
                send(7, part, 0, target, target, shifted(place, "core", 1))
    for part in every:
        copies[7, part, 0].wait_recv()
    for copy in copies.values():
        copy.wait_send()


def back(query_inner, passage_inner, normed, unit, scale, grad_unit, gain, bias, proj):
    spec = lambda space: pl.BlockSpec(memory_space=space)
    vm = lambda *shape: pltpu.VMEM(shape, bf16)
    vf = lambda *shape: pltpu.VMEM(shape, f32)
    r = PART_ROWS
    s = SIDE_ROWS
    return pl.pallas_call(
        back_kernel,
        out_shape=(
            jax.ShapeDtypeStruct((ROWS, HID), bf16),
            jax.ShapeDtypeStruct((PARTS, 2, r, DIM), bf16),
            jax.ShapeDtypeStruct((2, s, DIM), f32),
        ),
        in_specs=[spec(pl.ANY)] * 2 + [spec(pltpu.VMEM)] * 7,
        out_specs=(spec(pltpu.VMEM),) * 3,
        scratch_shapes=[
            vm(ROWS, FFW), vm(PARTS, 2, r, DIM), vf(2, s, DIM), vf(HID, DIM),
            vm(PARTS, r, DIM), vm(PARTS, r, DIM), vm(PARTS, 3, r // 4, DIM), vm(PARTS, r // 4, DIM),
            vm(PARTS, 3, r // 16, DIM), vm(PARTS, r // 16, DIM), vm(PARTS, 3, r // 64, DIM),
            vf(s, DIM), vf(s, DIM), vf(3, s // 4, DIM), vf(s // 4, DIM),
            vf(3, s // 16, DIM), vf(s // 16, DIM), vf(3, s // 64, DIM),
            pltpu.SemaphoreType.DMA((2,)),
            pltpu.SemaphoreType.DMA((8, PARTS + 1, 3)),
            pltpu.SemaphoreType.DMA((8, PARTS + 1, 3)),
        ],
        compiler_params=pltpu.CompilerParams(
            collective_id=3, has_side_effects=True, vmem_limit_bytes=58 * MIB
        ),
        name="back",
    )(query_inner, passage_inner, normed, unit, scale, grad_unit, gain, bias, proj)


def finish_kernel(grad_summed, weight, total, query_inner, passage_inner, query_resid, passage_resid, summed):
    i = pl.program_id(0)
    for part in range(PARTS):
        for h in range(2):
            column = part * 256 + h * DIM
            summed[:, column : column + DIM] = total[part, 0, h, 0].astype(f32)

    def inner_grad(ref):
        def block(n, carry):
            at = pl.ds(pl.multiple_of(n * HID, HID), HID)
            ref[:, at] = dot(grad_summed[...], weight[at, :], (1, 1)).astype(bf16)
            return carry

        lax.fori_loop(0, FFW // HID, block, 0)

    @pl.when(i == 0)
    def _():
        inner_grad(query_inner)
        query_resid[...] = grad_summed[...]

    @pl.when((i > 0) & (i < ROWS // CHUNK))
    def _():
        inner_grad(passage_inner)
        passage_resid[...] = grad_summed[...]


def finish(grad_summed, weight, total):
    steps = 6
    q_at = lambda i: (0, 0)
    p_at = lambda i: (jnp.clip(i - 1, 0, P_ROWS // CHUNK - 1), 0)
    return pl.pallas_call(
        finish_kernel,
        grid=(steps,),
        out_shape=(
            jax.ShapeDtypeStruct((Q_ROWS, FFW), bf16),
            jax.ShapeDtypeStruct((P_ROWS, FFW), bf16),
            jax.ShapeDtypeStruct((Q_ROWS, HID), bf16),
            jax.ShapeDtypeStruct((P_ROWS, HID), bf16),
            jax.ShapeDtypeStruct((FFW, HID), f32),
        ),
        in_specs=[
            pl.BlockSpec((CHUNK, HID), lambda i: (jnp.minimum(i, ROWS // CHUNK - 1), 0)),
            pl.BlockSpec((FFW, HID), lambda i: (0, 0)),
            pl.BlockSpec((PARTS, 1, 2, 1, 512, DIM), lambda i: (0, i // 3, 0, i % 3, 0, 0)),
        ],
        out_specs=(
            pl.BlockSpec((CHUNK, FFW), q_at),
            pl.BlockSpec((CHUNK, FFW), p_at),
            pl.BlockSpec((CHUNK, HID), q_at),
            pl.BlockSpec((CHUNK, HID), p_at),
            pl.BlockSpec((512, HID), lambda i: (i, 0)),
        ),
        compiler_params=pltpu.CompilerParams(vmem_limit_bytes=48 * MIB),
        name="finish",
    )(grad_summed, weight, total)


def ask_slots(negative_owner, negative_index):
    place = position()
    owner = negative_owner.reshape(-1)
    index = negative_index.reshape(-1)
    away = (
        ((owner // 32 + 4 - place["x"]) % 4) * 32
        + (((owner // 8) % 4 + 4 - place["z"]) % 4) * 8
        + (((owner // 4) % 2 + 2 - place["core"]) % 2) * 4
        + (owner % 4 + 4 - place["y"]) % 4
    )
    pair = jnp.arange(Q_DEV * NEG, dtype=jnp.int32)
    rank = jnp.sum(
        ((owner[None, :] == owner[:, None]) & (pair[None, :] < pair[:, None])).astype(jnp.int32), axis=1
    )
    slot_of = away * CAP + rank
    hit = slot_of[None, :] == jnp.arange(SLOTS, dtype=jnp.int32)[:, None]
    slot_query = jnp.sum(jnp.where(hit, pair // NEG, 0), axis=1)
    codes = Q_DEV + jnp.sum(jnp.where(hit, pair // NEG * 16 + index - Q_DEV, 0), axis=1)
    codes = jnp.pad(codes.reshape(DEVICES, 1, CAP), ((0, 0), (0, 0), (0, DIM - CAP)))
    return slot_query, slot_of, codes


def local(
    query_inner,
    query_resid,
    passage_inner,
    passage_resid,
    out_weight,
    norm_gain,
    norm_bias,
    proj_weight,
    negative_owner,
    negative_index,
):
    query_inner = query_inner.reshape(Q_ROWS, FFW)
    passage_inner = passage_inner.reshape(P_ROWS, FFW)
    gain = norm_gain.reshape(1, HID)
    bias = norm_bias.reshape(1, HID)
    slot_query, slot_of, codes = ask_slots(negative_owner, negative_index)
    normed, unit, scale, grad_unit, loss = pair_grads(
        slot_query, slot_of, codes, query_inner, query_resid.reshape(Q_ROWS, HID), passage_inner,
        passage_resid.reshape(P_ROWS, HID), out_weight, gain, bias, proj_weight,
    )
    grad_summed, total, side = back(
        query_inner, passage_inner, normed, unit, scale, grad_unit, gain, bias, proj_weight
    )
    grads = finish(grad_summed, out_weight, total.reshape(PARTS, 2, 2, 3, 512, DIM))
    side = side.reshape(2 * SIDE_ROWS, DIM)
    return (
        loss[:, 0],
        grads[0].reshape(Q_DEV, QLEN, FFW),
        grads[2].reshape(Q_DEV, QLEN, HID),
        grads[1].reshape(Q_DEV, PLEN, FFW),
        grads[3].reshape(Q_DEV, PLEN, HID),
        grads[4],
        side[:HID],
        side[HID : HID + 2 * HID // DIM].reshape(2, HID),
    )


def solution(mesh):
    in_specs = (
        P(("dp", "group"), None, None),
        P(("dp", "group"), None, None),
        P(("dp", "group"), None, None),
        P(("dp", "group"), None, None),
        P(),
        P(),
        P(),
        P(),
        P(("dp", "group"), None),
        P(("dp", "group"), None),
    )
    out_specs = (
        P(("dp", "group")),
        P(("dp", "group"), None, None),
        P(("dp", "group"), None, None),
        P(("dp", "group"), None, None),
        P(("dp", "group"), None, None),
        P(),
        P(),
        P(),
    )
    return jax.shard_map(local, mesh=mesh, in_specs=in_specs, out_specs=out_specs, check_vma=False)
```

```python
import functools

import jax
import jax.numpy as jnp
from jax import lax
from jax.experimental import pallas as pl
from jax.experimental.pallas import tpu as pltpu
from jax.sharding import PartitionSpec as P

HID = 768
FFW = 3072
DIM = 128
QLEN = 32
PLEN = 128
NEG = 16
Q_DEV = 8
DEVICES = 128
CAP = 2
Q_ROWS = Q_DEV * QLEN
P_ROWS = Q_DEV * PLEN
ROWS = Q_ROWS + P_ROWS
CHUNK = 256
SLOTS = DEVICES * CAP
BLOCKS = SLOTS // 8 + Q_DEV
SORTED = BLOCKS * 8
WIDE = 384
SPREAD = 37
SCORE_STEP = 4

MESH = pl.DeviceIdType.MESH
MIB = 1024 * 1024
bf16 = jnp.bfloat16
f32 = jnp.float32

pool_temp = 0.05
loss_scale = 1024.0
norm_eps = 1e-05
unit_eps = 1e-06

AXES = ("x", "y", "z")
ORDERS = (("x", "y", "z"), ("y", "z", "x"), ("z", "x", "y"), ("x", "y", "z"))
PARTS = 3
PART_ROWS = 3072
SIDE_ROWS = 512


def position():
    dp = lax.axis_index("dp")
    return {"x": dp // 8, "y": lax.axis_index("group"), "z": (dp // 2) % 4, "core": dp % 2}


def device_at(place):
    return ((place["x"] * 4 + place["z"]) * 2 + place["core"], place["y"])


def number_of(place):
    return place["x"] * 32 + place["z"] * 8 + place["core"] * 4 + place["y"]


def shifted(place, axis, step):
    return {**place, axis: (place[axis] + step) % (2 if axis == "core" else 4)}


def offset(place, t, sign):
    return {
        "x": (place["x"] + sign * (t // 32) + 4) % 4,
        "z": (place["z"] + sign * ((t // 8) % 4) + 4) % 4,
        "core": (place["core"] + sign * ((t // 4) % 2) + 2) % 2,
        "y": (place["y"] + sign * (t % 4) + 4) % 4,
    }


def dot(a, b, contract):
    return lax.dot_general(a, b, ((contract[:1], contract[1:]), ((), ())), preferred_element_type=f32)


def iota(shape, axis):
    return lax.broadcasted_iota(jnp.int32, shape, axis)


def count_of(mask, axis):
    return jnp.sum(jnp.where(mask, 1, 0), axis=axis, keepdims=True)


def pair_table(codes):
    passage = codes % 16
    sub = iota((SLOTS, 1), 0)
    slot = 2 * (sub % DEVICES) + sub // DEVICES
    square0, square1 = iota((SLOTS, SLOTS), 0), iota((SLOTS, SLOTS), 1)
    passage_row = jnp.sum(jnp.where(square0 == square1, passage, 0), axis=0, keepdims=True)
    rank = count_of((passage_row == passage) & (square1 < square0), 1)
    lane = iota((1, DIM), 1)
    blocks = jnp.where(lane < Q_DEV, (count_of(passage == lane, 0) + 7) // 8, 0)
    start = jnp.sum(jnp.where(lane < passage, blocks, 0), axis=1, keepdims=True)
    place = jnp.where(passage < Q_DEV, start * 8 + rank, SORTED)
    wide = iota((1, WIDE), 1)
    hit = (place == wide) & (wide < SORTED)
    order = jnp.sum(jnp.where(hit, slot - SLOTS, 0), axis=0, keepdims=True) + SLOTS
    order_sub = jnp.sum(jnp.where(hit, sub - SLOTS, 0), axis=0, keepdims=True) + SLOTS
    place_row = jnp.sum(jnp.where(slot == wide, place, 0), axis=0, keepdims=True)
    owner = jnp.zeros((1, WIDE), jnp.int32)
    goes_on = jnp.ones((1, WIDE), jnp.int32)
    last = jnp.zeros((1, WIDE), jnp.int32)
    for p in range(Q_DEV):
        begin = jnp.sum(jnp.where(lane < p, blocks, 0), axis=1, keepdims=True)
        end = jnp.sum(jnp.where(lane <= p, blocks, 0), axis=1, keepdims=True)
        owner += jnp.where(wide >= end, 1, 0)
        goes_on -= jnp.where((wide == begin) & (end > begin), 1, 0)
        last += jnp.where(wide == p, jnp.where(end > begin, end - 1, BLOCKS), 0)
    owner = jnp.minimum(owner, Q_DEV - 1)
    return jnp.concatenate([order, order_sub, place_row, owner, goes_on, last, last, last], axis=0)


def pool(query_side, passage_side):
    exp_logits = jnp.exp(dot(query_side, passage_side, (1, 1)) * (1.0 / pool_temp))
    totals = jnp.sum(exp_logits, axis=1, keepdims=True)
    weights = (exp_logits / totals).astype(bf16)
    queries = query_side.shape[0] // QLEN
    logs = jnp.broadcast_to(jnp.log(totals), (queries * QLEN, DIM)).reshape(queries, QLEN, DIM)
    return weights, pool_temp * jnp.sum(logs, axis=1)


def add_rows(out, out_at, terms, rows, chunk):
    def body(i, carry):
        at = pl.multiple_of(i * chunk, chunk)
        total = None
        for ref, start in terms:
            value = ref[pl.ds(pl.multiple_of(start + at, 8), chunk), :].astype(f32)
            total = value if total is None else total + value
        out[pl.ds(pl.multiple_of(out_at + at, 8), chunk), :] = total.astype(out.dtype)
        return carry

    lax.fori_loop(0, rows // chunk, body, 0)


def step_kernel(
    slot_query, slot_of, codes,
    query_inner, query_resid, passage_inner, passage_resid, out_weight, gain_in, bias_in, proj,
    grad_summed, out_ref, side_out, loss_out,
    gain, bias, inner, resid, weight, normed_out, unit_out, scale_out, grad_out,
    query_emb, passage_emb, codes_in, table, table_s,
    asks_out, asks_in, sorted_q, sorted_w, sorted_pull, sorted_exp, slot_exp, slot_seed, block_seed, chain,
    pulls_out, pulls_in, anchor_w, anchor_pull, anchor_score,
    sums, sums_in1, sums_in2,
    grad, side, proj_sum,
    core_in, held, in1, held1, in2, held2, in3,
    score_in, sheld, sin1, sheld1, sin2, sheld2, sin3,
    load_sem, table_sem, code_send, code_recv, ask_send, ask_recv, pull_send, pull_recv, sum_send, sum_recv,
    send_sem, recv_sem,
):
    place = position()
    core = place["core"]
    other = (core + 1) % 2
    me = number_of(place)
    lane_row = iota((1, DIM), 1)

    loads = [
        pltpu.make_async_copy(out_weight, weight, load_sem.at[0]),
        pltpu.make_async_copy(query_inner, inner.at[pl.ds(0, Q_ROWS)], load_sem.at[1]),
        pltpu.make_async_copy(query_resid, resid.at[pl.ds(0, Q_ROWS)], load_sem.at[2]),
        pltpu.make_async_copy(passage_inner, inner.at[pl.ds(Q_ROWS, P_ROWS)], load_sem.at[3]),
        pltpu.make_async_copy(passage_resid, resid.at[pl.ds(Q_ROWS, P_ROWS)], load_sem.at[4]),
    ]
    for load in loads:
        load.start()

    barrier = pltpu.get_barrier_semaphore()

    def greet(t, carry):
        pl.semaphore_signal(barrier, inc=1, device_id=device_at(offset(place, t, 1)), device_id_type=MESH)
        return carry

    lax.fori_loop(1, DEVICES, greet, 0)
    asks_in[SLOTS] = jnp.zeros((QLEN, DIM), bf16)
    sorted_pull[SORTED] = jnp.zeros((QLEN, DIM), bf16)
    sorted_exp[SORTED] = jnp.zeros((1, DIM), f32)
    slot_seed[SLOTS] = jnp.zeros((1, DIM), f32)
    chain[BLOCKS] = jnp.zeros((PLEN, DIM), f32)
    codes_in[0] = codes[0]
    gain[...] = gain_in[...].reshape(1, HID)
    bias[...] = bias_in[...].reshape(1, HID)
    proj_sum[...] = jnp.zeros_like(proj_sum)
    pl.semaphore_wait(barrier, DEVICES - 1)

    def code_copy(t):
        return pltpu.make_async_remote_copy(
            src_ref=codes.at[t], dst_ref=codes_in.at[t], send_sem=code_send, recv_sem=code_recv,
            device_id=device_at(offset(place, t, 1)), device_id_type=MESH,
        )

    def send_code(t, carry):
        code_copy(t).start()
        return carry

    lax.fori_loop(1, DEVICES, send_code, 0)

    def encode(at):
        at = pl.multiple_of(at, CHUNK)
        here = pl.ds(at, CHUNK)
        summed = dot(inner[here, :], weight[...], (1, 0)) + resid[here, :].astype(f32)
        center = summed - jnp.mean(summed, axis=1, keepdims=True)
        reciprocal = lax.rsqrt(jnp.mean(center * center, axis=1, keepdims=True) + norm_eps)
        normed = center * reciprocal
        normed_out[here, :] = normed
        layer_out = (normed * gain[...] + bias[...]).astype(bf16)
        projected = dot(layer_out, proj[...], (1, 0))
        length = jnp.sqrt(jnp.sum(projected * projected, axis=1, keepdims=True) + unit_eps)
        unit = projected / length
        unit_out[here, :] = unit
        scale_out[here, :] = jnp.where(iota((CHUNK, DIM), 1) < DIM // 2, reciprocal, length)
        return unit.astype(bf16)

    for load in loads[:3]:
        load.wait()
    query_emb[...] = encode(0).reshape(Q_DEV, QLEN, DIM)

    def ask_copy(t):
        rows = pl.ds(t * CAP, CAP)
        return pltpu.make_async_remote_copy(
            src_ref=asks_out.at[rows], dst_ref=asks_in.at[rows], send_sem=ask_send, recv_sem=ask_recv,
            device_id=device_at(offset(place, t, 1)), device_id_type=MESH,
        )

    def take_query(s):
        return query_emb[slot_query[s]]

    for r in range(CAP):
        asks_in[r] = take_query(r)

    def send_ask(i, carry):
        t = (i * SPREAD) % DEVICES
        for r in range(CAP):
            asks_out[t * CAP + r] = take_query(t * CAP + r)
        ask_copy(t).start()
        return carry

    lax.fori_loop(1, DEVICES, send_ask, 0)

    for load in loads[3:]:
        load.wait()

    def encode_passages(i, carry):
        passages = encode((i + 1) * CHUNK).reshape(CHUNK // PLEN, PLEN, DIM)
        passage_emb[pl.ds(i * (CHUNK // PLEN), CHUNK // PLEN)] = passages
        return carry

    lax.fori_loop(0, P_ROWS // CHUNK, encode_passages, 0)

    rest = pl.ds(1, DEVICES - 1)
    everyone = pltpu.make_async_remote_copy(
        src_ref=codes.at[rest], dst_ref=codes_in.at[rest], send_sem=code_send, recv_sem=code_recv,
        device_id=device_at(offset(place, 1, 1)), device_id_type=MESH,
    )
    everyone.wait()
    code_rows = codes_in[...].reshape(DEVICES, DIM)
    slot_codes = jnp.concatenate([code_rows[:, r : r + 1] for r in range(CAP)], axis=0)
    table[...] = pair_table(slot_codes)
    to_scalar = pltpu.make_async_copy(table, table_s, table_sem)
    to_scalar.start()

    def anchor(i, carry):
        rows = pl.ds(pl.multiple_of(i * QLEN, QLEN), QLEN)
        passage = passage_emb[i]
        weights, score = pool(query_emb[i], passage)
        anchor_w[rows, :] = weights
        anchor_pull[rows, :] = dot(weights, passage, (1, 0))
        anchor_score[pl.ds(i, 1), :] = score
        return carry

    lax.fori_loop(0, Q_DEV, anchor, 0)
    to_scalar.wait()

    def asked(buffer):
        return buffer.at[pl.ds(CAP, (DEVICES - 1) * CAP)]

    all_asks = pltpu.make_async_remote_copy(
        src_ref=asked(asks_out), dst_ref=asked(asks_in), send_sem=ask_send, recv_sem=ask_recv,
        device_id=device_at(offset(place, 1, 1)), device_id_type=MESH,
    )
    all_asks.wait()

    def score_blocks(n, carry):
        blocks = [n * SCORE_STEP + m for m in range(SCORE_STEP)]
        ats = [pl.multiple_of(b * CHUNK, CHUNK) for b in blocks]
        for b, at in zip(blocks, ats):
            for k in range(8):
                asking = asks_in[table_s[0, b * 8 + k]]
                sorted_q[pl.ds(pl.multiple_of(at + k * QLEN, QLEN), QLEN), :] = asking
        passages = [passage_emb[table_s[3, b]] for b in blocks]
        pooled = [pool(sorted_q[pl.ds(at, CHUNK), :], p) for at, p in zip(ats, passages)]
        pulls = [dot(weights, p, (1, 0)).reshape(8, QLEN, DIM) for (weights, _), p in zip(pooled, passages)]
        for b, at, (weights, score), pull in zip(blocks, ats, pooled, pulls):
            sorted_w[pl.ds(at, CHUNK), :] = weights
            exp_score = jnp.exp(score).reshape(8, 1, DIM)
            sorted_exp[pl.ds(b * 8, 8)] = exp_score
            sorted_pull[pl.ds(b * 8, 8)] = (pull * exp_score).astype(bf16)
        return carry

    lax.fori_loop(0, BLOCKS // SCORE_STEP, score_blocks, 0)

    def exp_of(t, carry):
        for r in range(CAP):
            slot_exp[pl.ds(r * DEVICES + t, 1), :] = sorted_exp[table_s[2, t * CAP + r]]
        return carry

    lax.fori_loop(0, DEVICES, exp_of, 0)

    t_col = iota((DEVICES, 1), 0)
    source = (
        ((place["x"] + 4 - t_col // 32) % 4) * 32
        + ((place["z"] + 4 - (t_col // 8) % 4) % 4) * 8
        + ((place["core"] + 2 - (t_col // 4) % 2) % 2) * 4
        + (place["y"] + 4 - t_col % 4) % 4
    )
    from_device = source == iota((DEVICES, DEVICES), 1)
    query_index = [(slot_codes[r * DEVICES : (r + 1) * DEVICES] // 16).astype(f32) for r in range(CAP)]
    eight = iota((Q_DEV, DIM), 0).astype(f32)
    own_exp = jnp.exp(anchor_score[...])
    spread = jnp.where(iota((Q_DEV, DIM), 1) == me, own_exp, 0.0)
    for r in range(CAP):
        exps = slot_exp[pl.ds(r * DEVICES, DEVICES), :]
        exp_row = jnp.sum(jnp.where(from_device, exps, 0.0), axis=0, keepdims=True)
        index_row = jnp.sum(jnp.where(from_device, query_index[r], 0.0), axis=0, keepdims=True)
        spread += jnp.where(eight == index_row, exp_row, 0.0)
    sums[0] = spread
    near, far = [], []
    for t in range(1, 8):
        peer = shifted(shifted(place, "core", t // 4), "y", t % 4)
        near.append(pltpu.make_async_remote_copy(
            src_ref=sums.at[0], dst_ref=sums_in1.at[t - 1], send_sem=sum_send.at[t - 1],
            recv_sem=sum_recv.at[t - 1], device_id=device_at(peer), device_id_type=MESH,
        ))
    for t in range(1, 16):
        peer = shifted(shifted(place, "x", t // 4), "z", t % 4)
        far.append(pltpu.make_async_remote_copy(
            src_ref=sums.at[1], dst_ref=sums_in2.at[t - 1], send_sem=sum_send.at[t + 6],
            recv_sem=sum_recv.at[t + 6], device_id=device_at(peer), device_id_type=MESH,
        ))
    for copy in near:
        copy.start()

    def pull_copy(t):
        rows = pl.ds(t * CAP, CAP)
        return pltpu.make_async_remote_copy(
            src_ref=pulls_out.at[rows], dst_ref=pulls_in.at[rows], send_sem=pull_send, recv_sem=pull_recv,
            device_id=device_at(offset(place, t, -1)), device_id_type=MESH,
        )

    def take_pull(s):
        return sorted_pull[table_s[2, s]]

    for copy in near:
        copy.wait_recv()
    sums[1] = sums[0] + jnp.sum(sums_in1[...], axis=0)
    for copy in far:
        copy.start()

    for r in range(CAP):
        pulls_in[r] = take_pull(r)

    def send_pull(i, carry):
        t = (i * SPREAD) % DEVICES
        for r in range(CAP):
            pulls_out[t * CAP + r] = take_pull(t * CAP + r)
        pull_copy(t).start()
        return carry

    lax.fori_loop(1, DEVICES, send_pull, 0)
    for copy in far:
        copy.wait_recv()
    total = sums[1] + jnp.sum(sums_in2[...], axis=0)

    for r in range(CAP):
        mine = jnp.zeros((DEVICES, DIM), f32)
        for i in range(Q_DEV):
            mine += jnp.where(from_device & (query_index[r] == float(i)), total[i : i + 1, :], 0.0)
        slot_total = jnp.sum(mine, axis=1, keepdims=True)
        here = pl.ds(r * DEVICES, DEVICES)
        slot_seed[here] = (loss_scale * (slot_exp[here, :] / slot_total)).reshape(DEVICES, 1, DIM)

    def push_block(b, carry):
        at = pl.multiple_of(b * CHUNK, CHUNK)
        for k in range(8):
            block_seed[pl.ds(k, 1), :] = slot_seed[table_s[1, b * 8 + k]]
        seeds = block_seed[...].reshape(8, 1, DIM)
        weights = sorted_w[pl.ds(at, CHUNK), :].astype(f32).reshape(8, QLEN, DIM) * seeds
        push = dot(weights.reshape(CHUNK, DIM).astype(bf16), sorted_q[pl.ds(at, CHUNK), :], (0, 0))
        goes_on = table_s[4, b].astype(f32)
        carry = carry * goes_on + push
        chain[b] = carry
        return carry

    lax.fori_loop(0, BLOCKS, push_block, jnp.zeros((PLEN, DIM), f32))

    own_total = jnp.sum(jnp.where(iota((Q_DEV, DIM), 1) == me, total, 0.0), axis=1, keepdims=True)
    own_total = jnp.broadcast_to(own_total, (Q_DEV, DIM))
    anchor_seed = loss_scale * (own_exp / own_total - 1.0)
    loss_out[...] = jnp.log(own_total) - anchor_score[...]
    for p in range(Q_DEV):
        push = dot(anchor_w[pl.ds(p * QLEN, QLEN), :], query_emb[p], (0, 0)) * anchor_seed[p : p + 1, :]
        push += chain[table_s[5, p]]
        grad_out[pl.ds(Q_ROWS + p * PLEN, PLEN), :] = push

    def back(i, carry):
        here = pl.ds(i * CHUNK if isinstance(i, int) else pl.multiple_of(i * CHUNK, CHUNK), CHUNK)
        u, g = unit_out[here, :], grad_out[here, :]
        reciprocal = scale_out[here, 0:1]
        length = scale_out[here, DIM - 1 : DIM]
        grad_projected = ((g - u * jnp.sum(u * g, axis=1, keepdims=True)) / length).astype(bf16)
        n = normed_out[here, :]
        layer_out = (n * gain[...] + bias[...]).astype(bf16)
        proj_sum[...] += dot(layer_out, grad_projected, (0, 0))
        grad_layer = dot(grad_projected, proj[...], (1, 1))
        norm_sums = (
            carry[0] + jnp.sum(grad_layer * n, axis=0, keepdims=True),
            carry[1] + jnp.sum(grad_layer, axis=0, keepdims=True),
        )
        grad_normed = grad_layer * gain[...]
        grad_summed[here, :] = (
            reciprocal
            * (
                grad_normed
                - jnp.mean(grad_normed, axis=1, keepdims=True)
                - n * jnp.mean(grad_normed * n, axis=1, keepdims=True)
            )
        ).astype(bf16)
        return norm_sums

    def weights(half, first, count, more):
        def block(g, carry):
            start = pl.multiple_of(half * (FFW // 2) + g * 512, 512)
            tokens = pl.ds(first, count)
            product = dot(inner[tokens, pl.ds(start, 512)], grad_summed[tokens, :], (0, 0))
            for part in range(PARTS):
                for h in range(2):
                    column = part * 256 + h * DIM
                    at = pl.ds(pl.multiple_of(h * (FFW // 2) + g * 512, 512), 512)
                    value = product[:, column : column + DIM]
                    if more:
                        value += grad[part, half, at, :].astype(f32)
                    grad[part, half, at, :] = value.astype(bf16)
            return carry

        lax.fori_loop(0, 3, block, 0)

    zero = jnp.zeros((1, HID), f32)
    norm_sums = lax.fori_loop(1, ROWS // CHUNK, back, (zero, zero))
    for half in range(2):
        weights(half, Q_ROWS, P_ROWS, False)

    pltpu.make_async_remote_copy(
        src_ref=asked(pulls_out), dst_ref=asked(pulls_in), send_sem=pull_send, recv_sem=pull_recv,
        device_id=device_at(offset(place, 1, 1)), device_id_type=MESH,
    ).wait()
    query_scale = loss_scale / own_total
    for i in range(Q_DEV):
        rows = pl.ds(i * QLEN, QLEN)
        pull = jnp.zeros((QLEN, DIM), f32)
        for k in range(NEG):
            pull += pulls_in[slot_of[i, k]].astype(f32)
        grad_out[rows, :] = (
            pull * query_scale[i : i + 1, :] + anchor_pull[rows, :] * anchor_seed[i : i + 1, :]
        )
    norm_sums = back(0, norm_sums)
    side[0] = proj_sum[0:SIDE_ROWS, :]
    side[1] = jnp.zeros((SIDE_ROWS, DIM), f32)
    side[1, 0 : HID - SIDE_ROWS, :] = proj_sum[SIDE_ROWS:HID, :]
    for n in range(2):
        for j in range(HID // DIM):
            row = HID - SIDE_ROWS + n * (HID // DIM) + j
            side[1, row : row + 1, :] = norm_sums[n][:, j * DIM : (j + 1) * DIM]

    copies = {}

    def send(phase, part, step, src, dst, peer):
        copy = pltpu.make_async_remote_copy(
            src_ref=src, dst_ref=dst,
            send_sem=send_sem.at[phase, part, step], recv_sem=recv_sem.at[phase, part, step],
            device_id=device_at(peer), device_id_type=MESH,
        )
        copy.start()
        copies[phase, part, step] = copy

    def bufs(part):
        if part < PARTS:
            return dict(
                src=grad.at[part], core_in=core_in.at[part], held=held.at[part],
                ins=(in1.at[part], in2.at[part], in3.at[part]),
                helds=(held1.at[part], held2.at[part]), out=out_ref.at[part], rows=PART_ROWS,
            )
        return dict(
            src=side, core_in=score_in, held=sheld, ins=(sin1, sin2, sin3),
            helds=(sheld1, sheld2), out=side_out, rows=SIDE_ROWS,
        )

    every = range(PARTS + 1)

    def send_half(part):
        b = bufs(part)
        send(0, part, 0, b["src"].at[other], b["core_in"], shifted(place, "core", 1))

    send_half(PARTS)
    weights(other, 0, Q_ROWS, True)
    for part in range(PARTS):
        send_half(part)
    weights(core, 0, Q_ROWS, True)

    for part in every:
        b = bufs(part)
        copies[0, part, 0].wait_recv()
        add_rows(b["held"], 0, [(b["src"].at[core], 0), (b["core_in"], 0)], b["rows"], 128)
        rows = b["rows"] // 4
        axis = ORDERS[part][0]
        for t in (1, 2, 3):
            peer = shifted(place, axis, t)
            at = pl.multiple_of(peer[axis] * rows, rows)
            send(1, part, t - 1, b["held"].at[pl.ds(at, rows)], b["ins"][0].at[t - 1], peer)
    for phase in (1, 2, 3):
        for part in every:
            b = bufs(part)
            rows = b["rows"] // 4**phase
            axis = ORDERS[part][phase - 1]
            here = b["held"] if phase == 1 else b["helds"][phase - 2]
            for t in (1, 2, 3):
                copies[phase, part, t - 1].wait_recv()
            terms = [(here, place[axis] * rows)] + [(b["ins"][phase - 1].at[t], 0) for t in range(3)]
            if phase < 3:
                target, at = b["helds"][phase - 1], 0
            else:
                target = b["out"].at[core]
                at = sum(place[a] * (b["rows"] // 4 ** (n + 1)) for n, a in enumerate(ORDERS[part]))
            add_rows(target, at, terms, rows, 96 if rows % 96 == 0 else min(rows, 64))
            if phase < 3:
                axis = ORDERS[part][phase]
                rows = rows // 4
                for t in (1, 2, 3):
                    peer = shifted(place, axis, t)
                    start = pl.multiple_of(peer[axis] * rows, rows)
                    send(phase + 1, part, t - 1, target.at[pl.ds(start, rows)], b["ins"][phase].at[t - 1], peer)
            else:
                axis = ORDERS[part][2]
                block = target.at[pl.ds(pl.multiple_of(at, 8 if part == PARTS else 16), rows)]
                for t in (1, 2, 3):
                    send(4, part, t - 1, block, block, shifted(place, axis, t))
    for phase in (4, 5, 6):
        for part in every:
            b = bufs(part)
            for t in (1, 2, 3):
                copies[phase, part, t - 1].wait_recv()
            target = b["out"].at[core]
            if phase < 6:
                depth = 6 - phase
                rows = b["rows"] // 4**depth
                axis = ORDERS[part][depth - 1]
                at = sum(
                    place[a] * (b["rows"] // 4 ** (n + 1)) for n, a in enumerate(ORDERS[part][:depth])
                )
                block = target.at[pl.ds(pl.multiple_of(at, 8 if part == PARTS else 16), rows)]
                for t in (1, 2, 3):
                    send(phase + 1, part, t - 1, block, block, shifted(place, axis, t))
            else:
                send(7, part, 0, target, target, shifted(place, "core", 1))
    for part in every:
        copies[7, part, 0].wait_recv()
    for copy in copies.values():
        copy.wait_send()
    for copy in near + far:
        copy.wait_send()


def step(slot_query, slot_of, codes, query_inner, query_resid, passage_inner, passage_resid,
         out_weight, gain, bias, proj):
    any_, vmem, smem = pl.ANY, pltpu.VMEM, pltpu.SMEM
    spec = lambda space: pl.BlockSpec(memory_space=space)
    dma = pltpu.SemaphoreType.DMA
    vm = lambda *shape: vmem(shape, bf16)
    vf = lambda *shape: vmem(shape, f32)
    r = PART_ROWS
    s = SIDE_ROWS
    return pl.pallas_call(
        step_kernel,
        out_shape=(
            jax.ShapeDtypeStruct((ROWS, HID), bf16),
            jax.ShapeDtypeStruct((PARTS, 2, r, DIM), bf16),
            jax.ShapeDtypeStruct((2, s, DIM), f32),
            jax.ShapeDtypeStruct((Q_DEV, DIM), f32),
        ),
        in_specs=[spec(smem), spec(smem), spec(vmem)] + [spec(any_)] * 5 + [spec(vmem)] * 3,
        out_specs=(spec(vmem),) * 4,
        scratch_shapes=[
            vf(1, HID), vf(1, HID),
            vm(ROWS, FFW), vm(ROWS, HID), vm(FFW, HID),
            vf(ROWS, HID), vf(ROWS, DIM), vf(ROWS, DIM), vf(ROWS, DIM),
            vm(Q_DEV, QLEN, DIM), vm(Q_DEV, PLEN, DIM),
            vmem((DEVICES, 1, DIM), jnp.int32), vmem((8, WIDE), jnp.int32), smem((8, WIDE), jnp.int32),
            vm(SLOTS, QLEN, DIM), vm(SLOTS + 1, QLEN, DIM),
            vm(SORTED * QLEN, DIM), vm(SORTED * QLEN, DIM), vm(SORTED + 1, QLEN, DIM),
            vf(SORTED + 1, 1, DIM), vf(SLOTS, DIM), vf(SLOTS + 1, 1, DIM), vf(8, DIM),
            vf(BLOCKS + 1, PLEN, DIM),
            vm(SLOTS, QLEN, DIM), vm(SLOTS, QLEN, DIM),
            vm(Q_ROWS, DIM), vf(Q_ROWS, DIM), vf(Q_DEV, DIM),
            vf(2, Q_DEV, DIM), vf(7, Q_DEV, DIM), vf(15, Q_DEV, DIM),
            vm(PARTS, 2, r, DIM), vf(2, s, DIM), vf(HID, DIM),
            vm(PARTS, r, DIM), vm(PARTS, r, DIM), vm(PARTS, 3, r // 4, DIM), vm(PARTS, r // 4, DIM),
            vm(PARTS, 3, r // 16, DIM), vm(PARTS, r // 16, DIM), vm(PARTS, 3, r // 64, DIM),
            vf(s, DIM), vf(s, DIM), vf(3, s // 4, DIM), vf(s // 4, DIM),
            vf(3, s // 16, DIM), vf(s // 16, DIM), vf(3, s // 64, DIM),
            dma((5,)), dma, dma, dma, dma, dma, dma, dma, dma((22,)), dma((22,)),
            dma((8, PARTS + 1, 3)), dma((8, PARTS + 1, 3)),
        ],
        compiler_params=pltpu.CompilerParams(
            collective_id=1, has_side_effects=True, vmem_limit_bytes=63 * MIB
        ),
        name="step",
    )(slot_query, slot_of, codes, query_inner, query_resid, passage_inner, passage_resid, out_weight,
      gain, bias, proj)


def finish_kernel(
    grad_summed, weight, total, side, loss,
    query_inner, passage_inner, query_resid, passage_resid, summed, proj_grad, norm_grad, query_loss,
):
    for part in range(PARTS):
        for h in range(2):
            column = part * 256 + h * DIM
            summed[:, column : column + DIM] = total[part, 0, h, 0].astype(f32)
    query_inner[...] = dot(grad_summed[0:Q_ROWS, :], weight[...], (1, 1)).astype(bf16)

    def block(n, carry):
        rows = pl.ds(pl.multiple_of(n * CHUNK, CHUNK), CHUNK)
        from_rows = pl.ds(pl.multiple_of(Q_ROWS + n * CHUNK, CHUNK), CHUNK)
        passage_inner[rows, :] = dot(grad_summed[from_rows, :], weight[...], (1, 1)).astype(bf16)
        return carry

    lax.fori_loop(0, P_ROWS // CHUNK, block, 0)

    @pl.when(pl.program_id(0) == 0)
    def _():
        query_resid[...] = grad_summed[0:Q_ROWS, :]
        passage_resid[...] = grad_summed[Q_ROWS:ROWS, :]
        proj_grad[0:SIDE_ROWS, :] = side[0]
        proj_grad[SIDE_ROWS:HID, :] = side[1, 0 : HID - SIDE_ROWS, :]
        for n in range(2):
            for j in range(HID // DIM):
                row = HID - SIDE_ROWS + n * (HID // DIM) + j
                norm_grad[n : n + 1, j * DIM : (j + 1) * DIM] = side[1, row : row + 1, :]
        for i in range(Q_DEV):
            query_loss[i] = loss[i, 0]


def finish(grad_summed, weight, total, side, loss):
    wide = 512
    whole = lambda *shape: pl.BlockSpec(shape, lambda i: (0,) * len(shape))
    return pl.pallas_call(
        finish_kernel,
        grid=(FFW // wide,),
        out_shape=(
            jax.ShapeDtypeStruct((Q_ROWS, FFW), bf16),
            jax.ShapeDtypeStruct((P_ROWS, FFW), bf16),
            jax.ShapeDtypeStruct((Q_ROWS, HID), bf16),
            jax.ShapeDtypeStruct((P_ROWS, HID), bf16),
            jax.ShapeDtypeStruct((FFW, HID), f32),
            jax.ShapeDtypeStruct((HID, DIM), f32),
            jax.ShapeDtypeStruct((2, HID), f32),
            jax.ShapeDtypeStruct((Q_DEV,), f32),
        ),
        in_specs=[
            whole(ROWS, HID),
            pl.BlockSpec((wide, HID), lambda i: (i, 0)),
            pl.BlockSpec((PARTS, 1, 2, 1, wide, DIM), lambda i: (0, i // 3, 0, i % 3, 0, 0)),
            whole(2, SIDE_ROWS, DIM),
            pl.BlockSpec(memory_space=pltpu.SMEM),
        ],
        out_specs=(
            pl.BlockSpec((Q_ROWS, wide), lambda i: (0, i)),
            pl.BlockSpec((P_ROWS, wide), lambda i: (0, i)),
            whole(Q_ROWS, HID),
            whole(P_ROWS, HID),
            pl.BlockSpec((wide, HID), lambda i: (i, 0)),
            whole(HID, DIM),
            whole(2, HID),
            pl.BlockSpec(memory_space=pltpu.SMEM),
        ),
        compiler_params=pltpu.CompilerParams(vmem_limit_bytes=48 * MIB),
        name="finish",
    )(grad_summed, weight, total, side, loss)


def ask_slots(negative_owner, negative_index):
    place = position()
    owner = negative_owner
    away = (
        ((owner // 32 + 4 - place["x"]) % 4) * 32
        + (((owner // 8) % 4 + 4 - place["z"]) % 4) * 8
        + (((owner // 4) % 2 + 2 - place["core"]) % 2) * 4
        + (owner % 4 + 4 - place["y"]) % 4
    )
    query = jnp.arange(Q_DEV, dtype=jnp.int32)
    same = owner[None, None] == owner[:, :, None, None]
    earlier = query[None, None, :, None] < query[:, None, None, None]
    rank = jnp.sum((same & earlier).astype(jnp.int32), axis=(2, 3))
    slot_of = away * CAP + rank
    hit = slot_of[None] == jnp.arange(SLOTS, dtype=jnp.int32)[:, None, None]
    slot_query = jnp.sum(jnp.where(hit, query[:, None], 0), axis=(1, 2))
    codes = Q_DEV + jnp.sum(jnp.where(hit, query[:, None] * 16 + negative_index - Q_DEV, 0), axis=(1, 2))
    codes = jnp.pad(codes.reshape(DEVICES, 1, CAP), ((0, 0), (0, 0), (0, DIM - CAP)))
    return slot_query, slot_of, codes


def local(
    query_inner,
    query_resid,
    passage_inner,
    passage_resid,
    out_weight,
    norm_gain,
    norm_bias,
    proj_weight,
    negative_owner,
    negative_index,
):
    query_inner = query_inner.reshape(Q_ROWS, FFW)
    passage_inner = passage_inner.reshape(P_ROWS, FFW)
    slot_query, slot_of, codes = ask_slots(negative_owner, negative_index)
    grad_summed, total, side, loss = step(
        slot_query, slot_of, codes, query_inner, query_resid.reshape(Q_ROWS, HID), passage_inner,
        passage_resid.reshape(P_ROWS, HID), out_weight, norm_gain, norm_bias, proj_weight,
    )
    grads = finish(grad_summed, out_weight, total.reshape(PARTS, 2, 2, 3, 512, DIM), side, loss)
    return (
        grads[7],
        grads[0].reshape(Q_DEV, QLEN, FFW),
        grads[2].reshape(Q_DEV, QLEN, HID),
        grads[1].reshape(Q_DEV, PLEN, FFW),
        grads[3].reshape(Q_DEV, PLEN, HID),
        grads[4],
        grads[5],
        grads[6],
    )


def solution(mesh):
    in_specs = (
        P(("dp", "group"), None, None),
        P(("dp", "group"), None, None),
        P(("dp", "group"), None, None),
        P(("dp", "group"), None, None),
        P(),
        P(),
        P(),
        P(),
        P(("dp", "group"), None),
        P(("dp", "group"), None),
    )
    out_specs = (
        P(("dp", "group")),
        P(("dp", "group"), None, None),
        P(("dp", "group"), None, None),
        P(("dp", "group"), None, None),
        P(("dp", "group"), None, None),
        P(),
        P(),
        P(),
    )
    return jax.shard_map(local, mesh=mesh, in_specs=in_specs, out_specs=out_specs, check_vma=False)
```

```python
import functools

import jax
import jax.numpy as jnp
from jax import lax
from jax.experimental import pallas as pl
from jax.experimental.pallas import tpu as pltpu
from jax.sharding import PartitionSpec as P

HID = 768
FFW = 3072
DIM = 128
QLEN = 32
PLEN = 128
NEG = 16
Q_DEV = 8
DEVICES = 128
CAP = 2
Q_ROWS = Q_DEV * QLEN
P_ROWS = Q_DEV * PLEN
ROWS = Q_ROWS + P_ROWS
CHUNK = 256
SLOTS = DEVICES * CAP
BLOCKS = SLOTS // 8 + Q_DEV
SORTED = BLOCKS * 8
WIDE = 384
SPREAD = 37
SCORE_STEP = 4

MESH = pl.DeviceIdType.MESH
MIB = 1024 * 1024
bf16 = jnp.bfloat16
f32 = jnp.float32

pool_temp = 0.05
loss_scale = 1024.0
norm_eps = 1e-05
unit_eps = 1e-06

AXES = ("x", "y", "z")
ORDERS = (("x", "y", "z"), ("y", "z", "x"), ("z", "x", "y"), ("x", "y", "z"))
PARTS = 3
PART_ROWS = 3072
SIDE_ROWS = 512
PIECES = [(part, first, rows) for first, rows in ((0, 2048), (2048, 1024)) for part in range(PARTS)]
PIECES += [(PARTS, 0, SIDE_ROWS)]


def position():
    dp = lax.axis_index("dp")
    return {"x": dp // 8, "y": lax.axis_index("group"), "z": (dp // 2) % 4, "core": dp % 2}


def device_at(place):
    return ((place["x"] * 4 + place["z"]) * 2 + place["core"], place["y"])


def number_of(place):
    return place["x"] * 32 + place["z"] * 8 + place["core"] * 4 + place["y"]


def shifted(place, axis, step):
    return {**place, axis: (place[axis] + step) % (2 if axis == "core" else 4)}


def offset(place, t, sign):
    return {
        "x": (place["x"] + sign * (t // 32) + 4) % 4,
        "z": (place["z"] + sign * ((t // 8) % 4) + 4) % 4,
        "core": (place["core"] + sign * ((t // 4) % 2) + 2) % 2,
        "y": (place["y"] + sign * (t % 4) + 4) % 4,
    }


def dot(a, b, contract):
    return lax.dot_general(a, b, ((contract[:1], contract[1:]), ((), ())), preferred_element_type=f32)


def iota(shape, axis):
    return lax.broadcasted_iota(jnp.int32, shape, axis)


def ask_plan(place, owner, index):
    away = (
        ((owner // 32 + 4 - place["x"]) % 4) * 32
        + (((owner // 8) % 4 + 4 - place["z"]) % 4) * 8
        + (((owner // 4) % 2 + 2 - place["core"]) % 2) * 4
        + (owner % 4 + 4 - place["y"]) % 4
    )
    lane = iota((Q_DEV, DIM), 1)
    asks = jnp.zeros((Q_DEV, DIM), jnp.int32)
    asked = jnp.zeros((Q_DEV, DIM), jnp.int32)
    for k in range(NEG):
        here = away[:, k : k + 1] == lane
        asks += jnp.where(here, 1, 0)
        asked += jnp.where(here, index[:, k : k + 1], 0)
    seen = jnp.zeros((1, DIM), jnp.int32)
    ranks = []
    for i in range(Q_DEV):
        ranks.append(seen)
        seen = seen + asks[i : i + 1]
    rank = jnp.concatenate(ranks, axis=0)
    slots = jnp.zeros((Q_DEV, DIM), jnp.int32)
    for k in range(NEG):
        column = away[:, k : k + 1]
        found = jnp.sum(jnp.where(column == lane, rank, 0), axis=1, keepdims=True)
        slots += jnp.where(lane == k, column * CAP + jnp.minimum(found, CAP - 1), 0)
    query = iota((Q_DEV, DIM), 0)
    square = iota((DEVICES, DIM), 0) == iota((DEVICES, DIM), 1)
    rows, columns = [], jnp.zeros((DEVICES, DIM), jnp.int32)
    for r in range(CAP):
        mine = (asks == 1) & (rank == r)
        rows.append(jnp.sum(jnp.where(mine, query, 0), axis=0, keepdims=True))
        code = Q_DEV + jnp.sum(jnp.where(mine, query * 16 + asked - Q_DEV, 0), axis=0, keepdims=True)
        column = jnp.sum(jnp.where(square, code, 0), axis=1, keepdims=True)
        columns += jnp.where(iota((DEVICES, DIM), 1) == r, column, 0)
    rows += [jnp.zeros((Q_DEV - CAP, DIM), jnp.int32), slots]
    return jnp.concatenate(rows, axis=0), columns


def count_of(mask, axis):
    return jnp.sum(jnp.where(mask, 1, 0), axis=axis, keepdims=True)


def pair_table(codes):
    passage = codes % 16
    sub = iota((SLOTS, 1), 0)
    slot = 2 * (sub % DEVICES) + sub // DEVICES
    square0, square1 = iota((SLOTS, SLOTS), 0), iota((SLOTS, SLOTS), 1)
    passage_row = jnp.sum(jnp.where(square0 == square1, passage, 0), axis=0, keepdims=True)
    rank = count_of((passage_row == passage) & (square1 < square0), 1)
    lane = iota((1, DIM), 1)
    blocks = jnp.where(lane < Q_DEV, (count_of(passage == lane, 0) + 7) // 8, 0)
    start = jnp.sum(jnp.where(lane < passage, blocks, 0), axis=1, keepdims=True)
    place = jnp.where(passage < Q_DEV, start * 8 + rank, SORTED)
    wide = iota((1, WIDE), 1)
    hit = (place == wide) & (wide < SORTED)
    order = jnp.sum(jnp.where(hit, slot - SLOTS, 0), axis=0, keepdims=True) + SLOTS
    order_sub = jnp.sum(jnp.where(hit, sub - SLOTS, 0), axis=0, keepdims=True) + SLOTS
    place_row = jnp.sum(jnp.where(slot == wide, place, 0), axis=0, keepdims=True)
    owner = jnp.zeros((1, WIDE), jnp.int32)
    goes_on = jnp.ones((1, WIDE), jnp.int32)
    last = jnp.zeros((1, WIDE), jnp.int32)
    for p in range(Q_DEV):
        begin = jnp.sum(jnp.where(lane < p, blocks, 0), axis=1, keepdims=True)
        end = jnp.sum(jnp.where(lane <= p, blocks, 0), axis=1, keepdims=True)
        owner += jnp.where(wide >= end, 1, 0)
        goes_on -= jnp.where((wide == begin) & (end > begin), 1, 0)
        last += jnp.where(wide == p, jnp.where(end > begin, end - 1, BLOCKS), 0)
    owner = jnp.minimum(owner, Q_DEV - 1)
    return jnp.concatenate([order, order_sub, place_row, owner, goes_on, last, last, last], axis=0)


def pool(query_side, passage_side):
    exp_logits = jnp.exp(dot(query_side, passage_side, (1, 1)) * (1.0 / pool_temp))
    totals = jnp.sum(exp_logits, axis=1, keepdims=True)
    weights = (exp_logits / totals).astype(bf16)
    queries = query_side.shape[0] // QLEN
    logs = jnp.broadcast_to(jnp.log(totals), (queries * QLEN, DIM)).reshape(queries, QLEN, DIM)
    return weights, pool_temp * jnp.sum(logs, axis=1)


def add_rows(out, out_at, terms, rows, chunk):
    def body(i, carry):
        at = pl.multiple_of(i * chunk, chunk)
        total = None
        for ref, start in terms:
            value = ref[pl.ds(pl.multiple_of(start + at, 8), chunk), :].astype(f32)
            total = value if total is None else total + value
        out[pl.ds(pl.multiple_of(out_at + at, 8), chunk), :] = total.astype(out.dtype)
        return carry

    lax.fori_loop(0, rows // chunk, body, 0)


def step_kernel(
    owners, indices,
    query_inner, query_resid, passage_inner, passage_resid, out_weight, gain_in, bias_in, proj,
    grad_hbm, out_hbm, side_hbm, loss_out,
    codes, codes_mid, plan, plan_s, grad_summed, out_ref, side_out, gain, bias, inner, resid, weight, normed_out, unit_out, scale_out, grad_out,
    query_emb, passage_emb, codes_in, table, table_s,
    asks_out, asks_in, sorted_q, sorted_w, sorted_pull, sorted_exp, slot_exp, slot_seed, block_seed, chain,
    pulls_out, pulls_in, anchor_w, anchor_pull, anchor_score,
    sums, sums_in1, sums_in2,
    grad, side, proj_sum,
    core_in, held, in1, held1, in2, held2, in3,
    score_in, sheld, sin1, sheld1, sin2, sheld2, sin3,
    load_sem, table_sem, store_sem, code_send, code_recv, ask_send, ask_recv, pull_send, pull_recv, sum_send, sum_recv,
    send_sem, recv_sem,
):
    place = position()
    core = place["core"]
    other = (core + 1) % 2
    me = number_of(place)
    lane_row = iota((1, DIM), 1)

    loads = [
        pltpu.make_async_copy(out_weight, weight, load_sem.at[0]),
        pltpu.make_async_copy(query_inner, inner.at[pl.ds(0, Q_ROWS)], load_sem.at[1]),
        pltpu.make_async_copy(query_resid, resid.at[pl.ds(0, Q_ROWS)], load_sem.at[2]),
        pltpu.make_async_copy(passage_inner, inner.at[pl.ds(Q_ROWS, P_ROWS)], load_sem.at[3]),
        pltpu.make_async_copy(passage_resid, resid.at[pl.ds(Q_ROWS, P_ROWS)], load_sem.at[4]),
    ]
    for load in loads:
        load.start()

    barrier = pltpu.get_barrier_semaphore()

    def greet(t, carry):
        pl.semaphore_signal(barrier, inc=1, device_id=device_at(offset(place, t, 1)), device_id_type=MESH)
        return carry

    lax.fori_loop(1, DEVICES, greet, 0)
    asks_in[SLOTS] = jnp.zeros((QLEN, DIM), bf16)
    sorted_pull[SORTED] = jnp.zeros((QLEN, DIM), bf16)
    sorted_exp[SORTED] = jnp.zeros((1, DIM), f32)
    slot_seed[SLOTS] = jnp.zeros((1, DIM), f32)
    chain[BLOCKS] = jnp.zeros((PLEN, DIM), f32)
    plan_rows, code_columns = ask_plan(place, owners[...], indices[...])
    plan[...] = plan_rows
    to_plan = pltpu.make_async_copy(plan, plan_s, table_sem)
    to_plan.start()
    codes[...] = code_columns.reshape(16, 8, 1, DIM)
    codes_mid[0] = codes[:, 0]
    gain[...] = gain_in[...].reshape(1, HID)
    bias[...] = bias_in[...].reshape(1, HID)
    proj_sum[...] = jnp.zeros_like(proj_sum)
    pl.semaphore_wait(barrier, DEVICES - 1)

    code_near, code_far = [], []
    for t in range(1, 8):
        peer = shifted(shifted(place, "core", t // 4), "y", t % 4)
        code_near.append(pltpu.make_async_remote_copy(
            src_ref=codes.at[:, t], dst_ref=codes_mid.at[t], send_sem=code_send.at[t - 1],
            recv_sem=code_recv.at[t - 1], device_id=device_at(peer), device_id_type=MESH,
        ))
    for t in range(1, 16):
        peer = shifted(shifted(place, "x", t // 4), "z", t % 4)
        code_far.append(pltpu.make_async_remote_copy(
            src_ref=codes_mid.at[:, t], dst_ref=codes_in.at[t], send_sem=code_send.at[t + 6],
            recv_sem=code_recv.at[t + 6], device_id=device_at(peer), device_id_type=MESH,
        ))
    for copy in code_near:
        copy.start()

    def encode(at):
        at = pl.multiple_of(at, CHUNK)
        here = pl.ds(at, CHUNK)
        summed = dot(inner[here, :], weight[...], (1, 0)) + resid[here, :].astype(f32)
        center = summed - jnp.mean(summed, axis=1, keepdims=True)
        reciprocal = lax.rsqrt(jnp.mean(center * center, axis=1, keepdims=True) + norm_eps)
        normed = center * reciprocal
        normed_out[here, :] = normed
        layer_out = (normed * gain[...] + bias[...]).astype(bf16)
        projected = dot(layer_out, proj[...], (1, 0))
        length = jnp.sqrt(jnp.sum(projected * projected, axis=1, keepdims=True) + unit_eps)
        unit = projected / length
        unit_out[here, :] = unit
        scale_out[here, :] = jnp.where(iota((CHUNK, DIM), 1) < DIM // 2, reciprocal, length)
        return unit.astype(bf16)

    to_plan.wait()
    for load in loads[:3]:
        load.wait()
    query_emb[...] = encode(0).reshape(Q_DEV, QLEN, DIM)
    for copy in code_near:
        copy.wait_recv()
    for copy in code_far:
        copy.start()
    codes_in[0] = codes_mid[:, 0]

    def ask_copy(t):
        rows = pl.ds(t * CAP, CAP)
        return pltpu.make_async_remote_copy(
            src_ref=asks_out.at[rows], dst_ref=asks_in.at[rows], send_sem=ask_send, recv_sem=ask_recv,
            device_id=device_at(offset(place, t, 1)), device_id_type=MESH,
        )

    def take_query(t, r):
        return query_emb[plan_s[r, t]]

    for r in range(CAP):
        asks_in[r] = take_query(0, r)

    def send_ask(i, carry):
        t = (i * SPREAD) % DEVICES
        for r in range(CAP):
            asks_out[t * CAP + r] = take_query(t, r)
        ask_copy(t).start()
        return carry

    lax.fori_loop(1, DEVICES, send_ask, 0)

    for load in loads[3:]:
        load.wait()

    def encode_passages(i, carry):
        passages = encode((i + 1) * CHUNK).reshape(CHUNK // PLEN, PLEN, DIM)
        passage_emb[pl.ds(i * (CHUNK // PLEN), CHUNK // PLEN)] = passages
        return carry

    lax.fori_loop(0, P_ROWS // CHUNK, encode_passages, 0)

    for copy in code_far:
        copy.wait_recv()
    code_rows = codes_in[...].reshape(DEVICES, DIM)
    slot_codes = jnp.concatenate([code_rows[:, r : r + 1] for r in range(CAP)], axis=0)
    table[...] = pair_table(slot_codes)
    to_scalar = pltpu.make_async_copy(table, table_s, table_sem)
    to_scalar.start()

    def anchor(i, carry):
        rows = pl.ds(pl.multiple_of(i * QLEN, QLEN), QLEN)
        passage = passage_emb[i]
        weights, score = pool(query_emb[i], passage)
        anchor_w[rows, :] = weights
        anchor_pull[rows, :] = dot(weights, passage, (1, 0))
        anchor_score[pl.ds(i, 1), :] = score
        return carry

    lax.fori_loop(0, Q_DEV, anchor, 0)
    to_scalar.wait()

    def asked(buffer):
        return buffer.at[pl.ds(CAP, (DEVICES - 1) * CAP)]

    all_asks = pltpu.make_async_remote_copy(
        src_ref=asked(asks_out), dst_ref=asked(asks_in), send_sem=ask_send, recv_sem=ask_recv,
        device_id=device_at(offset(place, 1, 1)), device_id_type=MESH,
    )
    all_asks.wait()

    def score_blocks(n, carry):
        blocks = [n * SCORE_STEP + m for m in range(SCORE_STEP)]
        ats = [pl.multiple_of(b * CHUNK, CHUNK) for b in blocks]
        for b, at in zip(blocks, ats):
            for k in range(8):
                asking = asks_in[table_s[0, b * 8 + k]]
                sorted_q[pl.ds(pl.multiple_of(at + k * QLEN, QLEN), QLEN), :] = asking
        passages = [passage_emb[table_s[3, b]] for b in blocks]
        pooled = [pool(sorted_q[pl.ds(at, CHUNK), :], p) for at, p in zip(ats, passages)]
        pulls = [dot(weights, p, (1, 0)).reshape(8, QLEN, DIM) for (weights, _), p in zip(pooled, passages)]
        for b, at, (weights, score), pull in zip(blocks, ats, pooled, pulls):
            sorted_w[pl.ds(at, CHUNK), :] = weights
            exp_score = jnp.exp(score).reshape(8, 1, DIM)
            sorted_exp[pl.ds(b * 8, 8)] = exp_score
            sorted_pull[pl.ds(b * 8, 8)] = (pull * exp_score).astype(bf16)
        return carry

    lax.fori_loop(0, BLOCKS // SCORE_STEP, score_blocks, 0)

    def exp_of(t, carry):
        for r in range(CAP):
            slot_exp[pl.ds(r * DEVICES + t, 1), :] = sorted_exp[table_s[2, t * CAP + r]]
        return carry

    lax.fori_loop(0, DEVICES, exp_of, 0)

    t_col = iota((DEVICES, 1), 0)
    source = (
        ((place["x"] + 4 - t_col // 32) % 4) * 32
        + ((place["z"] + 4 - (t_col // 8) % 4) % 4) * 8
        + ((place["core"] + 2 - (t_col // 4) % 2) % 2) * 4
        + (place["y"] + 4 - t_col % 4) % 4
    )
    from_device = source == iota((DEVICES, DEVICES), 1)
    query_index = [(slot_codes[r * DEVICES : (r + 1) * DEVICES] // 16).astype(f32) for r in range(CAP)]
    eight = iota((Q_DEV, DIM), 0).astype(f32)
    own_exp = jnp.exp(anchor_score[...])
    spread = jnp.where(iota((Q_DEV, DIM), 1) == me, own_exp, 0.0)
    for r in range(CAP):
        exps = slot_exp[pl.ds(r * DEVICES, DEVICES), :]
        exp_row = jnp.sum(jnp.where(from_device, exps, 0.0), axis=0, keepdims=True)
        index_row = jnp.sum(jnp.where(from_device, query_index[r], 0.0), axis=0, keepdims=True)
        spread += jnp.where(eight == index_row, exp_row, 0.0)
    sums[0] = spread
    near, far = [], []
    for t in range(1, 8):
        peer = shifted(shifted(place, "core", t // 4), "y", t % 4)
        near.append(pltpu.make_async_remote_copy(
            src_ref=sums.at[0], dst_ref=sums_in1.at[t - 1], send_sem=sum_send.at[t - 1],
            recv_sem=sum_recv.at[t - 1], device_id=device_at(peer), device_id_type=MESH,
        ))
    for t in range(1, 16):
        peer = shifted(shifted(place, "x", t // 4), "z", t % 4)
        far.append(pltpu.make_async_remote_copy(
            src_ref=sums.at[1], dst_ref=sums_in2.at[t - 1], send_sem=sum_send.at[t + 6],
            recv_sem=sum_recv.at[t + 6], device_id=device_at(peer), device_id_type=MESH,
        ))
    for copy in near:
        copy.start()

    def pull_copy(t):
        rows = pl.ds(t * CAP, CAP)
        return pltpu.make_async_remote_copy(
            src_ref=pulls_out.at[rows], dst_ref=pulls_in.at[rows], send_sem=pull_send, recv_sem=pull_recv,
            device_id=device_at(offset(place, t, -1)), device_id_type=MESH,
        )

    def take_pull(s):
        return sorted_pull[table_s[2, s]]

    for r in range(CAP):
        pulls_in[r] = take_pull(r)

    def gather_pull(t, carry):
        for r in range(CAP):
            pulls_out[t * CAP + r] = take_pull(t * CAP + r)
        return carry

    lax.fori_loop(1, DEVICES, gather_pull, 0, unroll=2)
    for copy in near:
        copy.wait_recv()
    sums[1] = sums[0] + jnp.sum(sums_in1[...], axis=0)
    for copy in far:
        copy.start()

    def send_pull(i, carry):
        pull_copy((i * SPREAD) % DEVICES).start()
        return carry

    lax.fori_loop(1, DEVICES, send_pull, 0)
    for copy in far:
        copy.wait_recv()
    total = sums[1] + jnp.sum(sums_in2[...], axis=0)

    for r in range(CAP):
        mine = jnp.zeros((DEVICES, DIM), f32)
        for i in range(Q_DEV):
            mine += jnp.where(from_device & (query_index[r] == float(i)), total[i : i + 1, :], 0.0)
        slot_total = jnp.sum(mine, axis=1, keepdims=True)
        here = pl.ds(r * DEVICES, DEVICES)
        slot_seed[here] = (loss_scale * (slot_exp[here, :] / slot_total)).reshape(DEVICES, 1, DIM)

    def push_block(b, carry):
        at = pl.multiple_of(b * CHUNK, CHUNK)
        for k in range(8):
            block_seed[pl.ds(k, 1), :] = slot_seed[table_s[1, b * 8 + k]]
        seeds = block_seed[...].reshape(8, 1, DIM)
        weights = sorted_w[pl.ds(at, CHUNK), :].astype(f32).reshape(8, QLEN, DIM) * seeds
        push = dot(weights.reshape(CHUNK, DIM).astype(bf16), sorted_q[pl.ds(at, CHUNK), :], (0, 0))
        goes_on = table_s[4, b].astype(f32)
        carry = carry * goes_on + push
        chain[b] = carry
        return carry

    lax.fori_loop(0, BLOCKS, push_block, jnp.zeros((PLEN, DIM), f32))

    own_total = jnp.sum(jnp.where(iota((Q_DEV, DIM), 1) == me, total, 0.0), axis=1, keepdims=True)
    own_total = jnp.broadcast_to(own_total, (Q_DEV, DIM))
    anchor_seed = loss_scale * (own_exp / own_total - 1.0)
    loss_out[...] = jnp.log(own_total) - anchor_score[...]
    for p in range(Q_DEV):
        push = dot(anchor_w[pl.ds(p * QLEN, QLEN), :], query_emb[p], (0, 0)) * anchor_seed[p : p + 1, :]
        push += chain[table_s[5, p]]
        grad_out[pl.ds(Q_ROWS + p * PLEN, PLEN), :] = push

    def back(i, carry):
        here = pl.ds(i * CHUNK if isinstance(i, int) else pl.multiple_of(i * CHUNK, CHUNK), CHUNK)
        u, g = unit_out[here, :], grad_out[here, :]
        reciprocal = scale_out[here, 0:1]
        length = scale_out[here, DIM - 1 : DIM]
        grad_projected = ((g - u * jnp.sum(u * g, axis=1, keepdims=True)) / length).astype(bf16)
        n = normed_out[here, :]
        layer_out = (n * gain[...] + bias[...]).astype(bf16)
        proj_sum[...] += dot(layer_out, grad_projected, (0, 0))
        grad_layer = dot(grad_projected, proj[...], (1, 1))
        norm_sums = (
            carry[0] + jnp.sum(grad_layer * n, axis=0, keepdims=True),
            carry[1] + jnp.sum(grad_layer, axis=0, keepdims=True),
        )
        grad_normed = grad_layer * gain[...]
        grad_summed[here, :] = (
            reciprocal
            * (
                grad_normed
                - jnp.mean(grad_normed, axis=1, keepdims=True)
                - n * jnp.mean(grad_normed * n, axis=1, keepdims=True)
            )
        ).astype(bf16)
        return norm_sums

    def weights(half, first, count, more):
        def block(g, carry):
            start = pl.multiple_of(half * (FFW // 2) + g * 512, 512)
            tokens = pl.ds(first, count)
            product = dot(inner[tokens, pl.ds(start, 512)], grad_summed[tokens, :], (0, 0))
            for part in range(PARTS):
                for h in range(2):
                    column = part * 256 + h * DIM
                    at = pl.ds(pl.multiple_of(h * (FFW // 2) + g * 512, 512), 512)
                    value = product[:, column : column + DIM]
                    if more:
                        value += grad[part, half, at, :].astype(f32)
                    grad[part, half, at, :] = value.astype(bf16)
            return carry

        lax.fori_loop(0, 3, block, 0)

    zero = jnp.zeros((1, HID), f32)
    norm_sums = lax.fori_loop(1, ROWS // CHUNK, back, (zero, zero))
    for half in range(2):
        weights(half, Q_ROWS, P_ROWS, False)

    pltpu.make_async_remote_copy(
        src_ref=asked(pulls_out), dst_ref=asked(pulls_in), send_sem=pull_send, recv_sem=pull_recv,
        device_id=device_at(offset(place, 1, 1)), device_id_type=MESH,
    ).wait()
    query_scale = loss_scale / own_total
    for i in range(Q_DEV):
        rows = pl.ds(i * QLEN, QLEN)
        pull = jnp.zeros((QLEN, DIM), f32)
        for k in range(NEG):
            pull += pulls_in[plan_s[8 + i, k]].astype(f32)
        grad_out[rows, :] = (
            pull * query_scale[i : i + 1, :] + anchor_pull[rows, :] * anchor_seed[i : i + 1, :]
        )
    norm_sums = back(0, norm_sums)
    stores = [pltpu.make_async_copy(grad_summed, grad_hbm, store_sem.at[len(PIECES), 0])]
    stores[0].start()
    side[0] = proj_sum[0:SIDE_ROWS, :]
    side[1] = jnp.zeros((SIDE_ROWS, DIM), f32)
    side[1, 0 : HID - SIDE_ROWS, :] = proj_sum[SIDE_ROWS:HID, :]
    for n in range(2):
        for j in range(HID // DIM):
            row = HID - SIDE_ROWS + n * (HID // DIM) + j
            side[1, row : row + 1, :] = norm_sums[n][:, j * DIM : (j + 1) * DIM]

    copies = {}

    def send(phase, part, step, src, dst, peer):
        copy = pltpu.make_async_remote_copy(
            src_ref=src, dst_ref=dst,
            send_sem=send_sem.at[phase, part, step], recv_sem=recv_sem.at[phase, part, step],
            device_id=device_at(peer), device_id_type=MESH,
        )
        copy.start()
        copies[phase, part, step] = copy

    def bufs(piece):
        part, first, rows = PIECES[piece]
        if part < PARTS:
            at = lambda n: pl.ds(first // n, rows // n)
            return dict(
                src=lambda half: grad.at[part, half, at(1)], hbm=lambda half: out_hbm.at[part, half, at(1)],
                core_in=core_in.at[part, at(1)], held=held.at[part, at(1)],
                ins=tuple(
                    (lambda t, ref=ref, n=n: ref.at[part, t, at(n)])
                    for ref, n in ((in1, 4), (in2, 16), (in3, 64))
                ),
                helds=(held1.at[part, at(4)], held2.at[part, at(16)]), out=out_ref.at[part, at(1)], rows=rows,
            )
        return dict(
            src=lambda half: side.at[half], hbm=lambda half: side_hbm.at[half], core_in=score_in, held=sheld,
            ins=tuple((lambda t, ref=ref: ref.at[t]) for ref in (sin1, sin2, sin3)),
            helds=(sheld1, sheld2), out=side_out, rows=rows,
        )

    every = range(len(PIECES))
    last = len(PIECES) - 1

    def send_half(part):
        b = bufs(part)
        send(0, part, 0, b["src"](other), b["core_in"], shifted(place, "core", 1))

    send_half(last)
    weights(other, 0, Q_ROWS, True)
    for part in range(last):
        send_half(part)
    weights(core, 0, Q_ROWS, True)

    for part in every:
        b = bufs(part)
        copies[0, part, 0].wait_recv()
        add_rows(b["held"], 0, [(b["src"](core), 0), (b["core_in"], 0)], b["rows"], 128)
        rows = b["rows"] // 4
        axis = ORDERS[PIECES[part][0]][0]
        for t in (1, 2, 3):
            peer = shifted(place, axis, t)
            at = pl.multiple_of(peer[axis] * rows, rows)
            send(1, part, t - 1, b["held"].at[pl.ds(at, rows)], b["ins"][0](t - 1), peer)
    for phase in (1, 2, 3):
        for part in every:
            b = bufs(part)
            rows = b["rows"] // 4**phase
            axis = ORDERS[PIECES[part][0]][phase - 1]
            here = b["held"] if phase == 1 else b["helds"][phase - 2]
            for t in (1, 2, 3):
                copies[phase, part, t - 1].wait_recv()
            terms = [(here, place[axis] * rows)] + [(b["ins"][phase - 1](t), 0) for t in range(3)]
            if phase < 3:
                target, at = b["helds"][phase - 1], 0
            else:
                target = b["out"]
                at = sum(place[a] * (b["rows"] // 4 ** (n + 1)) for n, a in enumerate(ORDERS[PIECES[part][0]]))
            add_rows(target, at, terms, rows, min(rows, 128))
            if phase < 3:
                axis = ORDERS[PIECES[part][0]][phase]
                rows = rows // 4
                for t in (1, 2, 3):
                    peer = shifted(place, axis, t)
                    start = pl.multiple_of(peer[axis] * rows, rows)
                    send(phase + 1, part, t - 1, target.at[pl.ds(start, rows)], b["ins"][phase](t - 1), peer)
            else:
                axis = ORDERS[PIECES[part][0]][2]
                block = target.at[pl.ds(pl.multiple_of(at, 8 if part == last else 16), rows)]
                for t in (1, 2, 3):
                    send(4, part, t - 1, block, block, shifted(place, axis, t))
    def hand_over(part, piece, at, rows):
        b = bufs(part)
        here = pl.ds(pl.multiple_of(at, rows), rows)
        send(7, part, piece, b["out"].at[here], b["hbm"](core).at[here], shifted(place, "core", 1))
        copy = pltpu.make_async_copy(b["out"].at[here], b["hbm"](core).at[here], store_sem.at[part, piece])
        copy.start()
        stores.append(copy)

    for phase in (4, 5):
        for part in every:
            b = bufs(part)
            for t in (1, 2, 3):
                copies[phase, part, t - 1].wait_recv()
            depth = 6 - phase
            rows = b["rows"] // 4**depth
            axis = ORDERS[PIECES[part][0]][depth - 1]
            at = sum(place[a] * (b["rows"] // 4 ** (n + 1)) for n, a in enumerate(ORDERS[PIECES[part][0]][:depth]))
            block = b["out"].at[pl.ds(pl.multiple_of(at, 8 if part == last else 16), rows)]
            for t in (1, 2, 3):
                send(phase + 1, part, t - 1, block, block, shifted(place, axis, t))
            if phase == 5:
                hand_over(part, 0, at, rows)
    for t in (1, 3, 2):
        for part in every:
            copies[6, part, t - 1].wait_recv()
            rows = bufs(part)["rows"] // 4
            axis = ORDERS[PIECES[part][0]][0]
            hand_over(part, t, shifted(place, axis, 4 - t)[axis] * rows, rows)
    for part in every:
        for piece in range(4):
            copies[7, part, piece].wait_recv()
    for copy in copies.values():
        copy.wait_send()
    for copy in stores:
        copy.wait()
    for copy in code_near + code_far + near + far:
        copy.wait_send()


def step(owners, indices, query_inner, query_resid, passage_inner, passage_resid, out_weight, gain, bias, proj):
    any_, vmem, smem = pl.ANY, pltpu.VMEM, pltpu.SMEM
    spec = lambda space: pl.BlockSpec(memory_space=space)
    dma = pltpu.SemaphoreType.DMA
    vm = lambda *shape: vmem(shape, bf16)
    vf = lambda *shape: vmem(shape, f32)
    r = PART_ROWS
    s = SIDE_ROWS
    return pl.pallas_call(
        step_kernel,
        out_shape=(
            jax.ShapeDtypeStruct((ROWS, HID), bf16),
            jax.ShapeDtypeStruct((PARTS, 2, r, DIM), bf16),
            jax.ShapeDtypeStruct((2, s, DIM), f32),
            jax.ShapeDtypeStruct((Q_DEV, DIM), f32),
        ),
        in_specs=[spec(vmem)] * 2 + [spec(any_)] * 5 + [spec(vmem)] * 3,
        out_specs=(spec(any_),) * 3 + (spec(vmem),),
        scratch_shapes=[
            vmem((16, 8, 1, DIM), jnp.int32), vmem((8, 16, 1, DIM), jnp.int32),
            vmem((16, DIM), jnp.int32), smem((16, DIM), jnp.int32),
            vm(ROWS, HID), vm(PARTS, r, DIM), vf(s, DIM),
            vf(1, HID), vf(1, HID),
            vm(ROWS, FFW), vm(ROWS, HID), vm(FFW, HID),
            vf(ROWS, HID), vf(ROWS, DIM), vf(ROWS, DIM), vf(ROWS, DIM),
            vm(Q_DEV, QLEN, DIM), vm(Q_DEV, PLEN, DIM),
            vmem((16, 8, 1, DIM), jnp.int32), vmem((8, WIDE), jnp.int32), smem((8, WIDE), jnp.int32),
            vm(SLOTS, QLEN, DIM), vm(SLOTS + 1, QLEN, DIM),
            vm(SORTED * QLEN, DIM), vm(SORTED * QLEN, DIM), vm(SORTED + 1, QLEN, DIM),
            vf(SORTED + 1, 1, DIM), vf(SLOTS, DIM), vf(SLOTS + 1, 1, DIM), vf(8, DIM),
            vf(BLOCKS + 1, PLEN, DIM),
            vm(SLOTS, QLEN, DIM), vm(SLOTS, QLEN, DIM),
            vm(Q_ROWS, DIM), vf(Q_ROWS, DIM), vf(Q_DEV, DIM),
            vf(2, Q_DEV, DIM), vf(7, Q_DEV, DIM), vf(15, Q_DEV, DIM),
            vm(PARTS, 2, r, DIM), vf(2, s, DIM), vf(HID, DIM),
            vm(PARTS, r, DIM), vm(PARTS, r, DIM), vm(PARTS, 3, r // 4, DIM), vm(PARTS, r // 4, DIM),
            vm(PARTS, 3, r // 16, DIM), vm(PARTS, r // 16, DIM), vm(PARTS, 3, r // 64, DIM),
            vf(s, DIM), vf(s, DIM), vf(3, s // 4, DIM), vf(s // 4, DIM),
            vf(3, s // 16, DIM), vf(s // 16, DIM), vf(3, s // 64, DIM),
            dma((5,)), dma, dma((len(PIECES) + 1, 4)), dma((22,)), dma((22,)), dma, dma, dma, dma, dma((22,)), dma((22,)),
            dma((8, len(PIECES), 4)), dma((8, len(PIECES), 4)),
        ],
        compiler_params=pltpu.CompilerParams(
            collective_id=1, has_side_effects=True, vmem_limit_bytes=63 * MIB
        ),
        name="step",
    )(owners, indices, query_inner, query_resid, passage_inner, passage_resid, out_weight, gain, bias, proj)


FINISH = 6
WIDE_ROWS = FFW // FINISH


def finish_kernel(
    grad_hbm, weight_hbm, total_hbm, side, loss,
    query_inner, passage_inner, query_resid, passage_resid, summed, proj_grad, norm_grad, query_loss,
    grad_summed, weight, total, inner, wide, load_sem, store_sem,
):
    loads = [pltpu.make_async_copy(grad_hbm, grad_summed, load_sem.at[0])]
    for n in range(FINISH):
        rows = pl.ds(n * WIDE_ROWS, WIDE_ROWS)
        loads.append(pltpu.make_async_copy(weight_hbm.at[rows], weight.at[rows], load_sem.at[1 + n]))
        loads.append(pltpu.make_async_copy(
            total_hbm.at[:, n // 3, :, n % 3], total.at[n], load_sem.at[1 + FINISH + n]
        ))
    for load in loads:
        load.start()
    stores = []

    def store(src, dst):
        copy = pltpu.make_async_copy(src, dst, store_sem.at[len(stores)])
        copy.start()
        stores.append(copy)

    proj_grad[0:SIDE_ROWS, :] = side[0]
    proj_grad[SIDE_ROWS:HID, :] = side[1, 0 : HID - SIDE_ROWS, :]
    for n in range(2):
        for j in range(HID // DIM):
            row = HID - SIDE_ROWS + n * (HID // DIM) + j
            norm_grad[n : n + 1, j * DIM : (j + 1) * DIM] = side[1, row : row + 1, :]
    for i in range(Q_DEV):
        query_loss[i] = loss[i, 0]
    loads[0].wait()
    store(grad_summed.at[pl.ds(0, Q_ROWS)], query_resid)
    store(grad_summed.at[pl.ds(Q_ROWS, P_ROWS)], passage_resid)
    for n in range(FINISH):
        rows = pl.ds(n * WIDE_ROWS, WIDE_ROWS)
        loads[1 + 2 * n].wait()

        inner[:, rows] = dot(grad_summed[...], weight[rows, :], (1, 1)).astype(bf16)
        store(inner.at[pl.ds(0, Q_ROWS), rows], query_inner.at[:, rows])
        store(inner.at[pl.ds(Q_ROWS, P_ROWS), rows], passage_inner.at[:, rows])
        loads[2 + 2 * n].wait()
        for part in range(PARTS):
            for h in range(2):
                column = part * 256 + h * DIM
                wide[rows, column : column + DIM] = total[n, part, h].astype(f32)
        store(wide.at[rows], summed.at[rows])
    for copy in stores:
        copy.wait()


def finish(grad_summed, weight, total, side, loss):
    spec = lambda space: pl.BlockSpec(memory_space=space)
    any_, vmem, smem = pl.ANY, pltpu.VMEM, pltpu.SMEM
    return pl.pallas_call(
        finish_kernel,
        out_shape=(
            jax.ShapeDtypeStruct((Q_ROWS, FFW), bf16),
            jax.ShapeDtypeStruct((P_ROWS, FFW), bf16),
            jax.ShapeDtypeStruct((Q_ROWS, HID), bf16),
            jax.ShapeDtypeStruct((P_ROWS, HID), bf16),
            jax.ShapeDtypeStruct((FFW, HID), f32),
            jax.ShapeDtypeStruct((HID, DIM), f32),
            jax.ShapeDtypeStruct((2, HID), f32),
            jax.ShapeDtypeStruct((Q_DEV,), f32),
        ),
        in_specs=[spec(any_)] * 3 + [spec(vmem), spec(smem)],
        out_specs=(spec(any_),) * 5 + (spec(vmem), spec(vmem), spec(smem)),
        scratch_shapes=[
            vmem((ROWS, HID), bf16),
            vmem((FFW, HID), bf16),
            vmem((FINISH, PARTS, 2, WIDE_ROWS, DIM), bf16),
            vmem((ROWS, FFW), bf16),
            vmem((FFW, HID), f32),
            pltpu.SemaphoreType.DMA((1 + 2 * FINISH,)),
            pltpu.SemaphoreType.DMA((2 + 3 * FINISH,)),
        ],
        compiler_params=pltpu.CompilerParams(vmem_limit_bytes=60 * MIB),
        name="finish",
    )(grad_summed, weight, total, side, loss)


def local(
    query_inner,
    query_resid,
    passage_inner,
    passage_resid,
    out_weight,
    norm_gain,
    norm_bias,
    proj_weight,
    negative_owner,
    negative_index,
):
    query_inner = query_inner.reshape(Q_ROWS, FFW)
    passage_inner = passage_inner.reshape(P_ROWS, FFW)
    grad_summed, total, side, loss = step(
        negative_owner, negative_index, query_inner, query_resid.reshape(Q_ROWS, HID), passage_inner,
        passage_resid.reshape(P_ROWS, HID), out_weight, norm_gain, norm_bias, proj_weight,
    )
    grads = finish(grad_summed, out_weight, total.reshape(PARTS, 2, 2, 3, 512, DIM), side, loss)
    return (
        grads[7],
        grads[0].reshape(Q_DEV, QLEN, FFW),
        grads[2].reshape(Q_DEV, QLEN, HID),
        grads[1].reshape(Q_DEV, PLEN, FFW),
        grads[3].reshape(Q_DEV, PLEN, HID),
        grads[4],
        grads[5],
        grads[6],
    )


def solution(mesh):
    in_specs = (
        P(("dp", "group"), None, None),
        P(("dp", "group"), None, None),
        P(("dp", "group"), None, None),
        P(("dp", "group"), None, None),
        P(),
        P(),
        P(),
        P(),
        P(("dp", "group"), None),
        P(("dp", "group"), None),
    )
    out_specs = (
        P(("dp", "group")),
        P(("dp", "group"), None, None),
        P(("dp", "group"), None, None),
        P(("dp", "group"), None, None),
        P(("dp", "group"), None, None),
        P(),
        P(),
        P(),
    )
    return jax.shard_map(local, mesh=mesh, in_specs=in_specs, out_specs=out_specs, check_vma=False)
```

```python
import functools

import jax
import jax.numpy as jnp
from jax import lax
from jax.experimental import pallas as pl
from jax.experimental.pallas import tpu as pltpu
from jax.sharding import PartitionSpec as P

HID = 768
FFW = 3072
DIM = 128
QLEN = 32
PLEN = 128
NEG = 16
Q_DEV = 8
DEVICES = 128
CAP = 2
Q_ROWS = Q_DEV * QLEN
P_ROWS = Q_DEV * PLEN
ROWS = Q_ROWS + P_ROWS
CHUNK = 256
SLOTS = DEVICES * CAP
BLOCKS = SLOTS // 8 + Q_DEV
SORTED = BLOCKS * 8
WIDE = 384
SPREAD = 37
SCORE_STEP = 4

MESH = pl.DeviceIdType.MESH
MIB = 1024 * 1024
bf16 = jnp.bfloat16
f32 = jnp.float32

pool_temp = 0.05
loss_scale = 1024.0
norm_eps = 1e-05
unit_eps = 1e-06

AXES = ("x", "y", "z")
ORDERS = (("x", "y", "z"), ("y", "z", "x"), ("z", "x", "y"), ("x", "y", "z"))
PARTS = 3
PART_ROWS = 3072
SIDE_ROWS = 512
PIECES = [(part, first, rows) for first, rows in ((0, 2048), (2048, 1024)) for part in range(PARTS)]
PIECES += [(PARTS, 0, SIDE_ROWS)]


def position():
    dp = lax.axis_index("dp")
    return {"x": dp // 8, "y": lax.axis_index("group"), "z": (dp // 2) % 4, "core": dp % 2}


def device_at(place):
    return ((place["x"] * 4 + place["z"]) * 2 + place["core"], place["y"])


def number_of(place):
    return place["x"] * 32 + place["z"] * 8 + place["core"] * 4 + place["y"]


def shifted(place, axis, step):
    return {**place, axis: (place[axis] + step) % (2 if axis == "core" else 4)}


def offset(place, t, sign):
    return {
        "x": lax.rem(place["x"] + sign * lax.div(t, 32) + 4, 4),
        "z": lax.rem(place["z"] + sign * lax.rem(lax.div(t, 8), 4) + 4, 4),
        "core": lax.rem(place["core"] + sign * lax.rem(lax.div(t, 4), 2) + 2, 2),
        "y": lax.rem(place["y"] + sign * lax.rem(t, 4) + 4, 4),
    }


def dot(a, b, contract):
    return lax.dot_general(a, b, ((contract[:1], contract[1:]), ((), ())), preferred_element_type=f32)


def iota(shape, axis):
    return lax.broadcasted_iota(jnp.int32, shape, axis)


def ask_plan(place, owner, index):
    away = (
        ((owner // 32 + 4 - place["x"]) % 4) * 32
        + (((owner // 8) % 4 + 4 - place["z"]) % 4) * 8
        + (((owner // 4) % 2 + 2 - place["core"]) % 2) * 4
        + (owner % 4 + 4 - place["y"]) % 4
    )
    lane = iota((Q_DEV, DIM), 1)
    asks = jnp.zeros((Q_DEV, DIM), jnp.int32)
    asked = jnp.zeros((Q_DEV, DIM), jnp.int32)
    for k in range(NEG):
        here = away[:, k : k + 1] == lane
        asks += jnp.where(here, 1, 0)
        asked += jnp.where(here, index[:, k : k + 1], 0)
    seen = jnp.zeros((1, DIM), jnp.int32)
    ranks = []
    for i in range(Q_DEV):
        ranks.append(seen)
        seen = seen + asks[i : i + 1]
    rank = jnp.concatenate(ranks, axis=0)
    slots = jnp.zeros((Q_DEV, DIM), jnp.int32)
    for k in range(NEG):
        column = away[:, k : k + 1]
        found = jnp.sum(jnp.where(column == lane, rank, 0), axis=1, keepdims=True)
        slots += jnp.where(lane == k, column * CAP + jnp.minimum(found, CAP - 1), 0)
    query = iota((Q_DEV, DIM), 0)
    square = iota((DEVICES, DIM), 0) == iota((DEVICES, DIM), 1)
    rows, columns = [], jnp.zeros((DEVICES, DIM), jnp.int32)
    for r in range(CAP):
        mine = (asks == 1) & (rank == r)
        rows.append(jnp.sum(jnp.where(mine, query, 0), axis=0, keepdims=True))
        code = Q_DEV + jnp.sum(jnp.where(mine, query * 16 + asked - Q_DEV, 0), axis=0, keepdims=True)
        column = jnp.sum(jnp.where(square, code, 0), axis=1, keepdims=True)
        columns += jnp.where(iota((DEVICES, DIM), 1) == r, column, 0)
    rows += [jnp.zeros((Q_DEV - CAP, DIM), jnp.int32), slots]
    return jnp.concatenate(rows, axis=0), columns


def count_of(mask, axis):
    return jnp.sum(jnp.where(mask, 1, 0), axis=axis, keepdims=True)


def pair_table(codes):
    passage = codes % 16
    sub = iota((SLOTS, 1), 0)
    slot = 2 * (sub % DEVICES) + sub // DEVICES
    square0, square1 = iota((SLOTS, SLOTS), 0), iota((SLOTS, SLOTS), 1)
    passage_row = jnp.sum(jnp.where(square0 == square1, passage, 0), axis=0, keepdims=True)
    rank = count_of((passage_row == passage) & (square1 < square0), 1)
    lane = iota((1, DIM), 1)
    blocks = jnp.where(lane < Q_DEV, (count_of(passage == lane, 0) + 7) // 8, 0)
    start = jnp.sum(jnp.where(lane < passage, blocks, 0), axis=1, keepdims=True)
    place = jnp.where(passage < Q_DEV, start * 8 + rank, SORTED)
    wide = iota((1, WIDE), 1)
    hit = (place == wide) & (wide < SORTED)
    order = jnp.sum(jnp.where(hit, slot - SLOTS, 0), axis=0, keepdims=True) + SLOTS
    order_sub = jnp.sum(jnp.where(hit, sub - SLOTS, 0), axis=0, keepdims=True) + SLOTS
    place_row = jnp.sum(jnp.where(slot == wide, place, 0), axis=0, keepdims=True)
    owner = jnp.zeros((1, WIDE), jnp.int32)
    goes_on = jnp.ones((1, WIDE), jnp.int32)
    last = jnp.zeros((1, WIDE), jnp.int32)
    for p in range(Q_DEV):
        begin = jnp.sum(jnp.where(lane < p, blocks, 0), axis=1, keepdims=True)
        end = jnp.sum(jnp.where(lane <= p, blocks, 0), axis=1, keepdims=True)
        owner += jnp.where(wide >= end, 1, 0)
        goes_on -= jnp.where((wide == begin) & (end > begin), 1, 0)
        last += jnp.where(wide == p, jnp.where(end > begin, end - 1, BLOCKS), 0)
    owner = jnp.minimum(owner, Q_DEV - 1)
    return jnp.concatenate([order, order_sub, place_row, owner, goes_on, last, last, last], axis=0)


def pool(query_side, passage_side):
    exp_logits = jnp.exp(dot(query_side, passage_side, (1, 1)) * (1.0 / pool_temp))
    totals = jnp.sum(exp_logits, axis=1, keepdims=True)
    weights = (exp_logits / totals).astype(bf16)
    queries = query_side.shape[0] // QLEN
    logs = jnp.broadcast_to(jnp.log(totals), (queries * QLEN, DIM)).reshape(queries, QLEN, DIM)
    return weights, pool_temp * jnp.sum(logs, axis=1)


def add_rows(out, out_at, terms, rows, chunk):
    def body(i, carry):
        at = pl.multiple_of(i * chunk, chunk)
        total = None
        for ref, start in terms:
            value = ref[pl.ds(pl.multiple_of(start + at, 8), chunk), :].astype(f32)
            total = value if total is None else total + value
        out[pl.ds(pl.multiple_of(out_at + at, 8), chunk), :] = total.astype(out.dtype)
        return carry

    lax.fori_loop(0, rows // chunk, body, 0)


def step_kernel(
    owners, indices,
    query_inner, query_resid, passage_inner, passage_resid, out_weight, gain_in, bias_in, proj,
    grad_hbm, out_hbm, side_hbm, loss_out,
    codes, codes_mid, plan, plan_s, grad_summed, out_ref, side_out, gain, bias, inner, resid, weight, normed_out, unit_out, scale_out, grad_out,
    query_emb, passage_emb, codes_in, table, table_s,
    asks_out, asks_in, sorted_q, sorted_w, sorted_pull, sorted_exp, slot_exp, slot_seed, block_seed, chain,
    pulls_out, pulls_in, anchor_w, anchor_pull, anchor_score,
    sums, sums_in1, sums_in2,
    grad, side, proj_sum,
    core_in, held, in1, held1, in2, held2, in3,
    score_in, sheld, sin1, sheld1, sin2, sheld2, sin3,
    load_sem, table_sem, store_sem, code_send, code_recv, ask_send, ask_recv, pull_send, pull_recv, sum_send, sum_recv,
    send_sem, recv_sem,
):
    place = position()
    core = place["core"]
    other = (core + 1) % 2
    me = number_of(place)
    lane_row = iota((1, DIM), 1)

    loads = [
        pltpu.make_async_copy(out_weight, weight, load_sem.at[0]),
        pltpu.make_async_copy(query_inner, inner.at[pl.ds(0, Q_ROWS)], load_sem.at[1]),
        pltpu.make_async_copy(query_resid, resid.at[pl.ds(0, Q_ROWS)], load_sem.at[2]),
        pltpu.make_async_copy(passage_inner, inner.at[pl.ds(Q_ROWS, P_ROWS)], load_sem.at[3]),
        pltpu.make_async_copy(passage_resid, resid.at[pl.ds(Q_ROWS, P_ROWS)], load_sem.at[4]),
    ]
    for load in loads:
        load.start()

    barrier = pltpu.get_barrier_semaphore()

    def greet(t, carry):
        pl.semaphore_signal(barrier, inc=1, device_id=device_at(offset(place, t, 1)), device_id_type=MESH)
        return carry

    lax.fori_loop(1, DEVICES, greet, 0, unroll=4)
    asks_in[SLOTS] = jnp.zeros((QLEN, DIM), bf16)
    sorted_pull[SORTED] = jnp.zeros((QLEN, DIM), bf16)
    sorted_exp[SORTED] = jnp.zeros((1, DIM), f32)
    slot_seed[SLOTS] = jnp.zeros((1, DIM), f32)
    chain[BLOCKS] = jnp.zeros((PLEN, DIM), f32)
    plan_rows, code_columns = ask_plan(place, owners[...], indices[...])
    plan[...] = plan_rows
    to_plan = pltpu.make_async_copy(plan, plan_s, table_sem)
    to_plan.start()
    codes[...] = code_columns.reshape(16, 8, 1, DIM)
    codes_mid[0] = codes[:, 0]
    gain[...] = gain_in[...].reshape(1, HID)
    bias[...] = bias_in[...].reshape(1, HID)
    proj_sum[...] = jnp.zeros_like(proj_sum)
    pl.semaphore_wait(barrier, DEVICES - 1)

    code_near, code_far = [], []
    for t in range(1, 8):
        peer = shifted(shifted(place, "core", t // 4), "y", t % 4)
        code_near.append(pltpu.make_async_remote_copy(
            src_ref=codes.at[:, t], dst_ref=codes_mid.at[t], send_sem=code_send.at[t - 1],
            recv_sem=code_recv.at[t - 1], device_id=device_at(peer), device_id_type=MESH,
        ))
    for t in range(1, 16):
        peer = shifted(shifted(place, "x", t // 4), "z", t % 4)
        code_far.append(pltpu.make_async_remote_copy(
            src_ref=codes_mid.at[:, t], dst_ref=codes_in.at[t], send_sem=code_send.at[t + 6],
            recv_sem=code_recv.at[t + 6], device_id=device_at(peer), device_id_type=MESH,
        ))
    for copy in code_near:
        copy.start()

    def encode(at):
        at = pl.multiple_of(at, CHUNK)
        here = pl.ds(at, CHUNK)
        summed = dot(inner[here, :], weight[...], (1, 0)) + resid[here, :].astype(f32)
        center = summed - jnp.mean(summed, axis=1, keepdims=True)
        reciprocal = lax.rsqrt(jnp.mean(center * center, axis=1, keepdims=True) + norm_eps)
        normed = center * reciprocal
        normed_out[here, :] = normed
        layer_out = (normed * gain[...] + bias[...]).astype(bf16)
        projected = dot(layer_out, proj[...], (1, 0))
        length = jnp.sqrt(jnp.sum(projected * projected, axis=1, keepdims=True) + unit_eps)
        unit = projected / length
        unit_out[here, :] = unit
        scale_out[here, :] = jnp.where(iota((CHUNK, DIM), 1) < DIM // 2, reciprocal, length)
        return unit.astype(bf16)

    to_plan.wait()
    for load in loads[:3]:
        load.wait()
    query_emb[...] = encode(0).reshape(Q_DEV, QLEN, DIM)
    for copy in code_near:
        copy.wait_recv()
    for copy in code_far:
        copy.start()
    codes_in[0] = codes_mid[:, 0]

    def ask_copy(t):
        rows = pl.ds(t * CAP, CAP)
        return pltpu.make_async_remote_copy(
            src_ref=asks_out.at[rows], dst_ref=asks_in.at[rows], send_sem=ask_send, recv_sem=ask_recv,
            device_id=device_at(offset(place, t, 1)), device_id_type=MESH,
        )

    def take_query(t, r):
        return query_emb[plan_s[r, t]]

    for r in range(CAP):
        asks_in[r] = take_query(0, r)

    def send_ask(i, carry):
        t = lax.rem(i * SPREAD, DEVICES)
        for r in range(CAP):
            asks_out[t * CAP + r] = take_query(t, r)
        ask_copy(t).start()
        return carry

    lax.fori_loop(1, DEVICES, send_ask, 0, unroll=2)

    for load in loads[3:]:
        load.wait()

    def encode_passages(i, carry):
        passages = encode((i + 1) * CHUNK).reshape(CHUNK // PLEN, PLEN, DIM)
        passage_emb[pl.ds(i * (CHUNK // PLEN), CHUNK // PLEN)] = passages
        return carry

    lax.fori_loop(0, P_ROWS // CHUNK, encode_passages, 0)

    for copy in code_far:
        copy.wait_recv()
    code_rows = codes_in[...].reshape(DEVICES, DIM)
    slot_codes = jnp.concatenate([code_rows[:, r : r + 1] for r in range(CAP)], axis=0)
    table[...] = pair_table(slot_codes)
    to_scalar = pltpu.make_async_copy(table, table_s, table_sem)
    to_scalar.start()

    def anchor(i, carry):
        rows = pl.ds(pl.multiple_of(i * QLEN, QLEN), QLEN)
        passage = passage_emb[i]
        weights, score = pool(query_emb[i], passage)
        anchor_w[rows, :] = weights
        anchor_pull[rows, :] = dot(weights, passage, (1, 0))
        anchor_score[pl.ds(i, 1), :] = score
        return carry

    lax.fori_loop(0, Q_DEV, anchor, 0)
    to_scalar.wait()

    def asked(buffer):
        return buffer.at[pl.ds(CAP, (DEVICES - 1) * CAP)]

    all_asks = pltpu.make_async_remote_copy(
        src_ref=asked(asks_out), dst_ref=asked(asks_in), send_sem=ask_send, recv_sem=ask_recv,
        device_id=device_at(shifted(place, "y", 1)), device_id_type=MESH,
    )
    all_asks.wait()

    def score_blocks(n, carry):
        blocks = [n * SCORE_STEP + m for m in range(SCORE_STEP)]
        ats = [pl.multiple_of(b * CHUNK, CHUNK) for b in blocks]
        for b, at in zip(blocks, ats):
            for k in range(8):
                asking = asks_in[table_s[0, b * 8 + k]]
                sorted_q[pl.ds(pl.multiple_of(at + k * QLEN, QLEN), QLEN), :] = asking
        passages = [passage_emb[table_s[3, b]] for b in blocks]
        pooled = [pool(sorted_q[pl.ds(at, CHUNK), :], p) for at, p in zip(ats, passages)]
        pulls = [dot(weights, p, (1, 0)).reshape(8, QLEN, DIM) for (weights, _), p in zip(pooled, passages)]
        for b, at, (weights, score), pull in zip(blocks, ats, pooled, pulls):
            sorted_w[pl.ds(at, CHUNK), :] = weights
            exp_score = jnp.exp(score).reshape(8, 1, DIM)
            sorted_exp[pl.ds(b * 8, 8)] = exp_score
            sorted_pull[pl.ds(b * 8, 8)] = (pull * exp_score).astype(bf16)
        return carry

    lax.fori_loop(0, BLOCKS // SCORE_STEP, score_blocks, 0)

    def exp_of(t, carry):
        for r in range(CAP):
            slot_exp[pl.ds(r * DEVICES + t, 1), :] = sorted_exp[table_s[2, t * CAP + r]]
        return carry

    lax.fori_loop(0, DEVICES, exp_of, 0, unroll=4)

    t_col = iota((DEVICES, 1), 0)
    source = (
        ((place["x"] + 4 - t_col // 32) % 4) * 32
        + ((place["z"] + 4 - (t_col // 8) % 4) % 4) * 8
        + ((place["core"] + 2 - (t_col // 4) % 2) % 2) * 4
        + (place["y"] + 4 - t_col % 4) % 4
    )
    from_device = source == iota((DEVICES, DEVICES), 1)
    query_index = [(slot_codes[r * DEVICES : (r + 1) * DEVICES] // 16).astype(f32) for r in range(CAP)]
    eight = iota((Q_DEV, DIM), 0).astype(f32)
    own_exp = jnp.exp(anchor_score[...])
    spread = jnp.where(iota((Q_DEV, DIM), 1) == me, own_exp, 0.0)
    for r in range(CAP):
        exps = slot_exp[pl.ds(r * DEVICES, DEVICES), :]
        exp_row = jnp.sum(jnp.where(from_device, exps, 0.0), axis=0, keepdims=True)
        index_row = jnp.sum(jnp.where(from_device, query_index[r], 0.0), axis=0, keepdims=True)
        spread += jnp.where(eight == index_row, exp_row, 0.0)
    sums[0] = spread
    near, far = [], []
    for t in range(1, 8):
        peer = shifted(shifted(place, "core", t // 4), "y", t % 4)
        near.append(pltpu.make_async_remote_copy(
            src_ref=sums.at[0], dst_ref=sums_in1.at[t - 1], send_sem=sum_send.at[t - 1],
            recv_sem=sum_recv.at[t - 1], device_id=device_at(peer), device_id_type=MESH,
        ))
    for t in range(1, 16):
        peer = shifted(shifted(place, "x", t // 4), "z", t % 4)
        far.append(pltpu.make_async_remote_copy(
            src_ref=sums.at[1], dst_ref=sums_in2.at[t - 1], send_sem=sum_send.at[t + 6],
            recv_sem=sum_recv.at[t + 6], device_id=device_at(peer), device_id_type=MESH,
        ))
    for copy in near:
        copy.start()

    def pull_copy(t):
        rows = pl.ds(t * CAP, CAP)
        return pltpu.make_async_remote_copy(
            src_ref=pulls_out.at[rows], dst_ref=pulls_in.at[rows], send_sem=pull_send, recv_sem=pull_recv,
            device_id=device_at(offset(place, t, -1)), device_id_type=MESH,
        )

    def take_pull(s):
        return sorted_pull[table_s[2, s]]

    for r in range(CAP):
        pulls_in[r] = take_pull(r)

    def gather_pull(t, carry):
        for r in range(CAP):
            pulls_out[t * CAP + r] = take_pull(t * CAP + r)
        return carry

    lax.fori_loop(1, DEVICES, gather_pull, 0, unroll=2)
    for copy in near:
        copy.wait_recv()
    sums[1] = sums[0] + jnp.sum(sums_in1[...], axis=0)
    for copy in far:
        copy.start()

    def send_pull(i, carry):
        pull_copy(lax.rem(i * SPREAD, DEVICES)).start()
        return carry

    lax.fori_loop(1, DEVICES, send_pull, 0, unroll=2)
    for copy in far:
        copy.wait_recv()
    total = sums[1] + jnp.sum(sums_in2[...], axis=0)

    for r in range(CAP):
        mine = jnp.zeros((DEVICES, DIM), f32)
        for i in range(Q_DEV):
            mine += jnp.where(from_device & (query_index[r] == float(i)), total[i : i + 1, :], 0.0)
        slot_total = jnp.sum(mine, axis=1, keepdims=True)
        here = pl.ds(r * DEVICES, DEVICES)
        slot_seed[here] = (loss_scale * (slot_exp[here, :] / slot_total)).reshape(DEVICES, 1, DIM)

    def push_block(b, carry):
        at = pl.multiple_of(b * CHUNK, CHUNK)
        for k in range(8):
            block_seed[pl.ds(k, 1), :] = slot_seed[table_s[1, b * 8 + k]]
        seeds = block_seed[...].reshape(8, 1, DIM)
        weights = sorted_w[pl.ds(at, CHUNK), :].astype(f32).reshape(8, QLEN, DIM) * seeds
        push = dot(weights.reshape(CHUNK, DIM).astype(bf16), sorted_q[pl.ds(at, CHUNK), :], (0, 0))
        goes_on = table_s[4, b].astype(f32)
        carry = carry * goes_on + push
        chain[b] = carry
        return carry

    lax.fori_loop(0, BLOCKS, push_block, jnp.zeros((PLEN, DIM), f32))

    own_total = jnp.sum(jnp.where(iota((Q_DEV, DIM), 1) == me, total, 0.0), axis=1, keepdims=True)
    own_total = jnp.broadcast_to(own_total, (Q_DEV, DIM))
    anchor_seed = loss_scale * (own_exp / own_total - 1.0)
    loss_out[...] = jnp.log(own_total) - anchor_score[...]
    for p in range(Q_DEV):
        push = dot(anchor_w[pl.ds(p * QLEN, QLEN), :], query_emb[p], (0, 0)) * anchor_seed[p : p + 1, :]
        push += chain[table_s[5, p]]
        grad_out[pl.ds(Q_ROWS + p * PLEN, PLEN), :] = push

    def back(i, carry):
        here = pl.ds(i * CHUNK if isinstance(i, int) else pl.multiple_of(i * CHUNK, CHUNK), CHUNK)
        u, g = unit_out[here, :], grad_out[here, :]
        reciprocal = scale_out[here, 0:1]
        length = scale_out[here, DIM - 1 : DIM]
        grad_projected = ((g - u * jnp.sum(u * g, axis=1, keepdims=True)) / length).astype(bf16)
        n = normed_out[here, :]
        layer_out = (n * gain[...] + bias[...]).astype(bf16)
        proj_sum[...] += dot(layer_out, grad_projected, (0, 0))
        grad_layer = dot(grad_projected, proj[...], (1, 1))
        norm_sums = (
            carry[0] + jnp.sum(grad_layer * n, axis=0, keepdims=True),
            carry[1] + jnp.sum(grad_layer, axis=0, keepdims=True),
        )
        grad_normed = grad_layer * gain[...]
        grad_summed[here, :] = (
            reciprocal
            * (
                grad_normed
                - jnp.mean(grad_normed, axis=1, keepdims=True)
                - n * jnp.mean(grad_normed * n, axis=1, keepdims=True)
            )
        ).astype(bf16)
        return norm_sums

    def weights(half, first, count, more):
        def block(g, carry):
            start = pl.multiple_of(half * (FFW // 2) + g * 512, 512)
            tokens = pl.ds(first, count)
            product = dot(inner[tokens, pl.ds(start, 512)], grad_summed[tokens, :], (0, 0))
            for part in range(PARTS):
                for h in range(2):
                    column = part * 256 + h * DIM
                    at = pl.ds(pl.multiple_of(h * (FFW // 2) + g * 512, 512), 512)
                    value = product[:, column : column + DIM]
                    if more:
                        value += grad[part, half, at, :].astype(f32)
                    grad[part, half, at, :] = value.astype(bf16)
            return carry

        lax.fori_loop(0, 3, block, 0)

    zero = jnp.zeros((1, HID), f32)
    norm_sums = lax.fori_loop(1, ROWS // CHUNK, back, (zero, zero))
    for half in range(2):
        weights(half, Q_ROWS, P_ROWS, False)

    pltpu.make_async_remote_copy(
        src_ref=asked(pulls_out), dst_ref=asked(pulls_in), send_sem=pull_send, recv_sem=pull_recv,
        device_id=device_at(shifted(place, "y", 1)), device_id_type=MESH,
    ).wait()
    query_scale = loss_scale / own_total
    for i in range(Q_DEV):
        rows = pl.ds(i * QLEN, QLEN)
        pull = jnp.zeros((QLEN, DIM), f32)
        for k in range(NEG):
            pull += pulls_in[plan_s[8 + i, k]].astype(f32)
        grad_out[rows, :] = (
            pull * query_scale[i : i + 1, :] + anchor_pull[rows, :] * anchor_seed[i : i + 1, :]
        )
    norm_sums = back(0, norm_sums)
    stores = [pltpu.make_async_copy(grad_summed, grad_hbm, store_sem.at[len(PIECES), 0])]
    stores[0].start()
    side[0] = proj_sum[0:SIDE_ROWS, :]
    side[1] = jnp.zeros((SIDE_ROWS, DIM), f32)
    side[1, 0 : HID - SIDE_ROWS, :] = proj_sum[SIDE_ROWS:HID, :]
    for n in range(2):
        for j in range(HID // DIM):
            row = HID - SIDE_ROWS + n * (HID // DIM) + j
            side[1, row : row + 1, :] = norm_sums[n][:, j * DIM : (j + 1) * DIM]

    copies = {}

    def send(phase, part, step, src, dst, peer):
        copy = pltpu.make_async_remote_copy(
            src_ref=src, dst_ref=dst,
            send_sem=send_sem.at[phase, part, step], recv_sem=recv_sem.at[phase, part, step],
            device_id=device_at(peer), device_id_type=MESH,
        )
        copy.start()
        copies[phase, part, step] = copy

    def bufs(piece):
        part, first, rows = PIECES[piece]
        if part < PARTS:
            at = lambda n: pl.ds(first // n, rows // n)
            return dict(
                src=lambda half: grad.at[part, half, at(1)], hbm=lambda half: out_hbm.at[part, half, at(1)],
                core_in=core_in.at[part, at(1)], held=held.at[part, at(1)],
                ins=tuple(
                    (lambda t, ref=ref, n=n: ref.at[part, t, at(n)])
                    for ref, n in ((in1, 4), (in2, 16), (in3, 64))
                ),
                helds=(held1.at[part, at(4)], held2.at[part, at(16)]), out=out_ref.at[part, at(1)], rows=rows,
            )
        return dict(
            src=lambda half: side.at[half], hbm=lambda half: side_hbm.at[half], core_in=score_in, held=sheld,
            ins=tuple((lambda t, ref=ref: ref.at[t]) for ref in (sin1, sin2, sin3)),
            helds=(sheld1, sheld2), out=side_out, rows=rows,
        )

    every = range(len(PIECES))
    last = len(PIECES) - 1

    def send_half(part):
        b = bufs(part)
        send(0, part, 0, b["src"](other), b["core_in"], shifted(place, "core", 1))

    send_half(last)
    weights(other, 0, Q_ROWS, True)
    for part in range(last):
        send_half(part)
    weights(core, 0, Q_ROWS, True)

    for part in every:
        b = bufs(part)
        copies[0, part, 0].wait_recv()
        add_rows(b["held"], 0, [(b["src"](core), 0), (b["core_in"], 0)], b["rows"], 128)
        rows = b["rows"] // 4
        axis = ORDERS[PIECES[part][0]][0]
        for t in (1, 2, 3):
            peer = shifted(place, axis, t)
            at = pl.multiple_of(peer[axis] * rows, rows)
            send(1, part, t - 1, b["held"].at[pl.ds(at, rows)], b["ins"][0](t - 1), peer)
    for phase in (1, 2, 3):
        for part in every:
            b = bufs(part)
            rows = b["rows"] // 4**phase
            axis = ORDERS[PIECES[part][0]][phase - 1]
            here = b["held"] if phase == 1 else b["helds"][phase - 2]
            for t in (1, 2, 3):
                copies[phase, part, t - 1].wait_recv()
            terms = [(here, place[axis] * rows)] + [(b["ins"][phase - 1](t), 0) for t in range(3)]
            if phase < 3:
                target, at = b["helds"][phase - 1], 0
            else:
                target = b["out"]
                at = sum(place[a] * (b["rows"] // 4 ** (n + 1)) for n, a in enumerate(ORDERS[PIECES[part][0]]))
            add_rows(target, at, terms, rows, min(rows, 128))
            if phase < 3:
                axis = ORDERS[PIECES[part][0]][phase]
                rows = rows // 4
                for t in (1, 2, 3):
                    peer = shifted(place, axis, t)
                    start = pl.multiple_of(peer[axis] * rows, rows)
                    send(phase + 1, part, t - 1, target.at[pl.ds(start, rows)], b["ins"][phase](t - 1), peer)
            else:
                axis = ORDERS[PIECES[part][0]][2]
                block = target.at[pl.ds(pl.multiple_of(at, 8 if part == last else 16), rows)]
                for t in (1, 2, 3):
                    send(4, part, t - 1, block, block, shifted(place, axis, t))
    def hand_over(part, piece, at, rows):
        b = bufs(part)
        here = pl.ds(pl.multiple_of(at, rows), rows)
        send(7, part, piece, b["out"].at[here], b["hbm"](core).at[here], shifted(place, "core", 1))
        copy = pltpu.make_async_copy(b["out"].at[here], b["hbm"](core).at[here], store_sem.at[part, piece])
        copy.start()
        stores.append(copy)

    for phase in (4, 5):
        for part in every:
            b = bufs(part)
            for t in (1, 2, 3):
                copies[phase, part, t - 1].wait_recv()
            depth = 6 - phase
            rows = b["rows"] // 4**depth
            axis = ORDERS[PIECES[part][0]][depth - 1]
            at = sum(place[a] * (b["rows"] // 4 ** (n + 1)) for n, a in enumerate(ORDERS[PIECES[part][0]][:depth]))
            block = b["out"].at[pl.ds(pl.multiple_of(at, 8 if part == last else 16), rows)]
            for t in (1, 2, 3):
                send(phase + 1, part, t - 1, block, block, shifted(place, axis, t))
            if phase == 5:
                hand_over(part, 0, at, rows)
    for t in (1, 3, 2):
        for part in every:
            copies[6, part, t - 1].wait_recv()
            rows = bufs(part)["rows"] // 4
            axis = ORDERS[PIECES[part][0]][0]
            hand_over(part, t, shifted(place, axis, 4 - t)[axis] * rows, rows)
    for part in every:
        for piece in range(4):
            copies[7, part, piece].wait_recv()
    for copy in copies.values():
        copy.wait_send()
    for copy in stores:
        copy.wait()
    for copy in code_near + code_far + near + far:
        copy.wait_send()


def step(owners, indices, query_inner, query_resid, passage_inner, passage_resid, out_weight, gain, bias, proj):
    any_, vmem, smem = pl.ANY, pltpu.VMEM, pltpu.SMEM
    spec = lambda space: pl.BlockSpec(memory_space=space)
    dma = pltpu.SemaphoreType.DMA
    vm = lambda *shape: vmem(shape, bf16)
    vf = lambda *shape: vmem(shape, f32)
    r = PART_ROWS
    s = SIDE_ROWS
    return pl.pallas_call(
        step_kernel,
        out_shape=(
            jax.ShapeDtypeStruct((ROWS, HID), bf16),
            jax.ShapeDtypeStruct((PARTS, 2, r, DIM), bf16),
            jax.ShapeDtypeStruct((2, s, DIM), f32),
            jax.ShapeDtypeStruct((Q_DEV, DIM), f32),
        ),
        in_specs=[spec(vmem)] * 2 + [spec(any_)] * 5 + [spec(vmem)] * 3,
        out_specs=(spec(any_),) * 3 + (spec(vmem),),
        scratch_shapes=[
            vmem((16, 8, 1, DIM), jnp.int32), vmem((8, 16, 1, DIM), jnp.int32),
            vmem((16, DIM), jnp.int32), smem((16, DIM), jnp.int32),
            vm(ROWS, HID), vm(PARTS, r, DIM), vf(s, DIM),
            vf(1, HID), vf(1, HID),
            vm(ROWS, FFW), vm(ROWS, HID), vm(FFW, HID),
            vf(ROWS, HID), vf(ROWS, DIM), vf(ROWS, DIM), vf(ROWS, DIM),
            vm(Q_DEV, QLEN, DIM), vm(Q_DEV, PLEN, DIM),
            vmem((16, 8, 1, DIM), jnp.int32), vmem((8, WIDE), jnp.int32), smem((8, WIDE), jnp.int32),
            vm(SLOTS, QLEN, DIM), vm(SLOTS + 1, QLEN, DIM),
            vm(SORTED * QLEN, DIM), vm(SORTED * QLEN, DIM), vm(SORTED + 1, QLEN, DIM),
            vf(SORTED + 1, 1, DIM), vf(SLOTS, DIM), vf(SLOTS + 1, 1, DIM), vf(8, DIM),
            vf(BLOCKS + 1, PLEN, DIM),
            vm(SLOTS, QLEN, DIM), vm(SLOTS, QLEN, DIM),
            vm(Q_ROWS, DIM), vf(Q_ROWS, DIM), vf(Q_DEV, DIM),
            vf(2, Q_DEV, DIM), vf(7, Q_DEV, DIM), vf(15, Q_DEV, DIM),
            vm(PARTS, 2, r, DIM), vf(2, s, DIM), vf(HID, DIM),
            vm(PARTS, r, DIM), vm(PARTS, r, DIM), vm(PARTS, 3, r // 4, DIM), vm(PARTS, r // 4, DIM),
            vm(PARTS, 3, r // 16, DIM), vm(PARTS, r // 16, DIM), vm(PARTS, 3, r // 64, DIM),
            vf(s, DIM), vf(s, DIM), vf(3, s // 4, DIM), vf(s // 4, DIM),
            vf(3, s // 16, DIM), vf(s // 16, DIM), vf(3, s // 64, DIM),
            dma((5,)), dma, dma((len(PIECES) + 1, 4)), dma((22,)), dma((22,)), dma, dma, dma, dma, dma((22,)), dma((22,)),
            dma((8, len(PIECES), 4)), dma((8, len(PIECES), 4)),
        ],
        compiler_params=pltpu.CompilerParams(
            collective_id=1, has_side_effects=True, vmem_limit_bytes=63 * MIB
        ),
        name="step",
    )(owners, indices, query_inner, query_resid, passage_inner, passage_resid, out_weight, gain, bias, proj)


FINISH = 6
WIDE_ROWS = FFW // FINISH


def finish_kernel(
    grad_hbm, weight_hbm, total_hbm, side, loss,
    query_inner, passage_inner, query_resid, passage_resid, summed, proj_grad, norm_grad, query_loss,
    grad_summed, weight, total, inner, wide, load_sem, store_sem,
):
    loads = [pltpu.make_async_copy(grad_hbm, grad_summed, load_sem.at[0])]
    for n in range(FINISH):
        rows = pl.ds(n * WIDE_ROWS, WIDE_ROWS)
        loads.append(pltpu.make_async_copy(weight_hbm.at[rows], weight.at[rows], load_sem.at[1 + n]))
        loads.append(pltpu.make_async_copy(
            total_hbm.at[:, n // 3, :, n % 3], total.at[n], load_sem.at[1 + FINISH + n]
        ))
    for load in loads:
        load.start()
    stores = []

    def store(src, dst):
        copy = pltpu.make_async_copy(src, dst, store_sem.at[len(stores)])
        copy.start()
        stores.append(copy)

    proj_grad[0:SIDE_ROWS, :] = side[0]
    proj_grad[SIDE_ROWS:HID, :] = side[1, 0 : HID - SIDE_ROWS, :]
    for n in range(2):
        for j in range(HID // DIM):
            row = HID - SIDE_ROWS + n * (HID // DIM) + j
            norm_grad[n : n + 1, j * DIM : (j + 1) * DIM] = side[1, row : row + 1, :]
    for i in range(Q_DEV):
        query_loss[i] = loss[i, 0]
    loads[0].wait()
    store(grad_summed.at[pl.ds(0, Q_ROWS)], query_resid)
    store(grad_summed.at[pl.ds(Q_ROWS, P_ROWS)], passage_resid)
    for n in range(FINISH):
        rows = pl.ds(n * WIDE_ROWS, WIDE_ROWS)
        loads[1 + 2 * n].wait()

        inner[:, rows] = dot(grad_summed[...], weight[rows, :], (1, 1)).astype(bf16)
        store(inner.at[pl.ds(0, Q_ROWS), rows], query_inner.at[:, rows])
        store(inner.at[pl.ds(Q_ROWS, P_ROWS), rows], passage_inner.at[:, rows])
        loads[2 + 2 * n].wait()
        for part in range(PARTS):
            for h in range(2):
                column = part * 256 + h * DIM
                wide[rows, column : column + DIM] = total[n, part, h].astype(f32)
        store(wide.at[rows], summed.at[rows])
    for copy in stores:
        copy.wait()


def finish(grad_summed, weight, total, side, loss):
    spec = lambda space: pl.BlockSpec(memory_space=space)
    any_, vmem, smem = pl.ANY, pltpu.VMEM, pltpu.SMEM
    return pl.pallas_call(
        finish_kernel,
        out_shape=(
            jax.ShapeDtypeStruct((Q_ROWS, FFW), bf16),
            jax.ShapeDtypeStruct((P_ROWS, FFW), bf16),
            jax.ShapeDtypeStruct((Q_ROWS, HID), bf16),
            jax.ShapeDtypeStruct((P_ROWS, HID), bf16),
            jax.ShapeDtypeStruct((FFW, HID), f32),
            jax.ShapeDtypeStruct((HID, DIM), f32),
            jax.ShapeDtypeStruct((2, HID), f32),
            jax.ShapeDtypeStruct((Q_DEV,), f32),
        ),
        in_specs=[spec(any_)] * 3 + [spec(vmem), spec(smem)],
        out_specs=(spec(any_),) * 5 + (spec(vmem), spec(vmem), spec(smem)),
        scratch_shapes=[
            vmem((ROWS, HID), bf16),
            vmem((FFW, HID), bf16),
            vmem((FINISH, PARTS, 2, WIDE_ROWS, DIM), bf16),
            vmem((ROWS, FFW), bf16),
            vmem((FFW, HID), f32),
            pltpu.SemaphoreType.DMA((1 + 2 * FINISH,)),
            pltpu.SemaphoreType.DMA((2 + 3 * FINISH,)),
        ],
        compiler_params=pltpu.CompilerParams(vmem_limit_bytes=60 * MIB),
        name="finish",
    )(grad_summed, weight, total, side, loss)


def local(
    query_inner,
    query_resid,
    passage_inner,
    passage_resid,
    out_weight,
    norm_gain,
    norm_bias,
    proj_weight,
    negative_owner,
    negative_index,
):
    query_inner = query_inner.reshape(Q_ROWS, FFW)
    passage_inner = passage_inner.reshape(P_ROWS, FFW)
    grad_summed, total, side, loss = step(
        negative_owner, negative_index, query_inner, query_resid.reshape(Q_ROWS, HID), passage_inner,
        passage_resid.reshape(P_ROWS, HID), out_weight, norm_gain, norm_bias, proj_weight,
    )
    grads = finish(grad_summed, out_weight, total.reshape(PARTS, 2, 2, 3, 512, DIM), side, loss)
    return (
        grads[7],
        grads[0].reshape(Q_DEV, QLEN, FFW),
        grads[2].reshape(Q_DEV, QLEN, HID),
        grads[1].reshape(Q_DEV, PLEN, FFW),
        grads[3].reshape(Q_DEV, PLEN, HID),
        grads[4],
        grads[5],
        grads[6],
    )


def solution(mesh):
    in_specs = (
        P(("dp", "group"), None, None),
        P(("dp", "group"), None, None),
        P(("dp", "group"), None, None),
        P(("dp", "group"), None, None),
        P(),
        P(),
        P(),
        P(),
        P(("dp", "group"), None),
        P(("dp", "group"), None),
    )
    out_specs = (
        P(("dp", "group")),
        P(("dp", "group"), None, None),
        P(("dp", "group"), None, None),
        P(("dp", "group"), None, None),
        P(("dp", "group"), None, None),
        P(),
        P(),
        P(),
    )
    return jax.shard_map(local, mesh=mesh, in_specs=in_specs, out_specs=out_specs, check_vma=False)
```
